32 devices in a mesh: elec: 8 (over y, x, core), drop: 4 (over z).
Axes of the slice: x: 2, y: 2, z: 4, core: 2. Of those that a mesh axis runs over, the one named last changes fastest.
Arguments:
- elec_pos: float32 [3, 4096], P(None, 'elec'), may hold values from -3 to 3
- drop_vert: float32 [3, 4096], P(None, 'drop'), may hold values from -4 to 4
- drop_conn: int32 [3, 8192], P(None, 'drop'), may hold values from 0 to 4095, as said below
- elec_rhs: float32 [128, 4096], P(None, 'elec'), may hold values from -6 to 6
- drop_rhs: float32 [128, 8192], P(None, 'drop'), may hold values from -6 to 6
- elec_inv: float32 [32, 128, 128], P('elec')
- drop_inv: float32 [64, 128, 128], P('drop')
Outputs:
- charge_elec: float32 [128, 4096], P(None, 'elec')
- charge_drop: float32 [128, 8192], P(None, 'drop')
The draws below stay inside these ranges and needn't reach their ends.
Inputs may be any that keep to these rules, and one draw needn't show every extreme that they name: `drop_conn`: panel p's three vertices all lie in vertex block p // 2048, that is among vertices (1024) * (p // 2048) to 1024 * (p // 2048 + 1) - 1; every vertex is the first vertex of exactly two panels of its block.
All inputs are finite; a program needn't handle non-finite values.
Results may differ from the reference program's by a relative error of at most 0.0001.
Values sent between devices are 32-bit elements; how exact they have to be, the bound alone decides.
No kernel may reach another device: no remote copies, remote signals or barrier semaphores. Data moves between devices by JAX's collectives and lax.ppermute only.
A program may use at most 64 MiB of HBM per device.

```python
import math
import jax
import jax.numpy as jnp
from jax import lax

ND_DEV = 2048
R = 128
BS = 128
ITERS = 2
NE = 4096
ND = 8192
NV = 4096


def inverse_blocks(key, block_count):
    first, second = jax.random.split(key)
    diagonal = jax.random.uniform(first, (block_count, BS), jnp.float32, 0.6, 1.6)
    noise = jax.random.normal(second, (block_count, BS, BS), jnp.float32) * (0.5 / math.sqrt(BS))
    return noise + diagonal[:, :, None] * jnp.eye(BS, dtype=jnp.float32)


def draw_elec_inv(key, part):
    return inverse_blocks(jax.random.fold_in(key, 21), NE // BS)


def draw_drop_inv(key, part):
    return inverse_blocks(jax.random.fold_in(key, 23), ND // BS)


def draw_drop_conn(key, part):
    block_count = ND // ND_DEV
    half_block = ND_DEV // 2
    perm_keys = jax.random.split(jax.random.fold_in(key, 11), 2 * block_count)
    firsts = jax.vmap(lambda single: jax.random.permutation(single, half_block))(perm_keys)
    firsts = firsts.astype(jnp.int32).reshape(1, block_count, ND_DEV)
    others = jax.random.randint(jax.random.fold_in(key, 13), (2, block_count, ND_DEV), 0, half_block, dtype=jnp.int32)
    offsets = (jnp.arange(block_count, dtype=jnp.int32) * half_block)[None, :, None]
    stacked = jnp.concatenate([firsts, others], axis=0) + offsets
    return stacked.reshape(3, ND)


def block_scale(key, extent, cuts, low, high):
    level = 1.0
    for axis_at, blocks in cuts:
        draws = jax.random.uniform(jax.random.fold_in(jax.random.fold_in(key, 6), axis_at), (blocks,), jnp.float32, low / len(cuts), high / len(cuts))
        level = level * jnp.repeat(jnp.exp(draws), extent[axis_at] // blocks).reshape((-1,) + (1,) * (len(extent) - 1 - axis_at))
    return level


def normal_values(rng, extent, spread, bound, shards=(), held_as=jnp.bfloat16):
    loudness = block_scale(rng, extent, shards, -0.22, 0.18) if shards else 1.0
    array = jax.random.normal(rng, extent, jnp.float32) * spread * loudness
    return jnp.minimum(jnp.maximum(array, -bound), bound).astype(held_as)


def setup_inputs(seed: int = 0) -> dict:
    arg_keys = jax.random.split(jax.random.key(seed), 8)
    return {
        "elec_pos": normal_values(arg_keys[0], (3, NE), 0.7, 3.0, ((1, 8),), jnp.float32),
        "drop_vert": normal_values(arg_keys[1], (3, NV), 1.0, 4.0, ((1, 4),), jnp.float32),
        "drop_conn": draw_drop_conn(jax.random.fold_in(arg_keys[7], 71), 0),
        "elec_rhs": normal_values(arg_keys[3], (R, NE), 1.0, 6.0, ((1, 8),), jnp.float32),
        "drop_rhs": normal_values(arg_keys[4], (R, ND), 1.0, 6.0, ((1, 4),), jnp.float32),
        "elec_inv": draw_elec_inv(jax.random.fold_in(arg_keys[7], 71), 0),
        "drop_inv": draw_drop_inv(jax.random.fold_in(arg_keys[7], 71), 0),
    }


HIGH = lax.Precision.HIGHEST

def constants(total_drop):
    screen = 1.0
    soften = 0.001
    couple = 1.0 / (3.0 * math.sqrt(total_drop))
    return (screen, soften, couple)

def centroids(drop_vert, conn):
    corners = jnp.take(drop_vert, conn, axis=1)
    return (corners[:, 0] + corners[:, 1] + corners[:, 2]) / 3.0

def kernel_tile(position, centres, screen, soften, couple):
    delta_x = position[0][:, None] - centres[0][None, :]
    delta_y = position[1][:, None] - centres[1][None, :]
    delta_z = position[2][:, None] - centres[2][None, :]
    distance = jnp.sqrt(delta_x * delta_x + delta_y * delta_y + delta_z * delta_z + soften)
    return couple * jnp.exp(-screen * distance) / distance

def block_solve(inverse, values):
    rhs_rows, columns = values.shape
    block_count, block_size, _ = inverse.shape
    shaped = values.reshape(rhs_rows, block_count, block_size)
    solved = jnp.einsum('bjk,rbk->rbj', inverse, shaped, precision=HIGH)
    return solved.reshape(rhs_rows, columns)

def reference(elec_pos, drop_vert, drop_conn, elec_rhs, drop_rhs, elec_inv, drop_inv):
    screen, soften, couple = constants(ND)
    centres = centroids(drop_vert, drop_conn)
    block_rows = math.gcd(NE, 512)
    block_count = NE // block_rows
    elec_blocks = jnp.moveaxis(elec_pos.reshape(3, block_count, block_rows), 1, 0)

    def cross(charge_elec, charge_drop):
        charge_blocks = jnp.moveaxis(charge_elec.reshape(R, block_count, block_rows), 1, 0)

        def visit_block(summed, inputs):
            position, charge_part = inputs
            kernel = kernel_tile(position, centres, screen, soften, couple)
            to_elec = lax.dot_general(charge_drop, kernel, (((1,), (1,)), ((), ())), precision=HIGH)
            summed = summed + jnp.dot(charge_part, kernel, precision=HIGH)
            return (summed, to_elec)
        field_drop, pieces = lax.scan(visit_block, jnp.zeros((R, ND), jnp.float32), (elec_blocks, charge_blocks))
        field_elec = jnp.moveaxis(pieces, 0, 1).reshape(R, NE)
        return (field_elec, field_drop)
    charge_elec = block_solve(elec_inv, elec_rhs)
    charge_drop = block_solve(drop_inv, drop_rhs)
    for iteration in range(ITERS):
        field_elec, field_drop = cross(charge_elec, charge_drop)
        charge_elec = block_solve(elec_inv, elec_rhs - field_elec)
        charge_drop = block_solve(drop_inv, drop_rhs - field_drop)
    return (charge_elec, charge_drop)
```

```python
import math

import jax
import jax.numpy as jnp
from jax import lax
from jax.experimental import pallas as pl
from jax.experimental.pallas import tpu as pltpu
from jax.sharding import PartitionSpec as P

SOFTEN = 0.001
SCREEN = 1.0
LANES = 128
CHUNK = 256
VMEM = pl.BlockSpec(memory_space=pltpu.VMEM)
SMEM = pl.BlockSpec(memory_space=pltpu.SMEM)
PARAMS = pltpu.CompilerParams(vmem_limit_bytes=40 * 2**20)
ROWS_IN = ((1,), (0,))
ROWS_OUT = ((1,), (1,))


def couple_of(total_drop):
    return 1.0 / (3.0 * math.sqrt(total_drop))


def split(value):
    high = value.astype(jnp.bfloat16)
    low = (value - high.astype(jnp.float32)).astype(jnp.bfloat16)
    return high, low


def stacked(value):
    high, low = split(value)
    return high, jnp.concatenate([high, low], axis=0)


def product(charge, weights, contract):
    high, both = charge
    weight_high, weight_low = weights
    dims = (contract, ((), ()))
    first = lax.dot_general(both, weight_high, dims, preferred_element_type=jnp.float32)
    second = lax.dot_general(high, weight_low, dims, preferred_element_type=jnp.float32)
    rows = high.shape[0]
    return first[:rows] + (first[rows:] + second)


def solve_block(inverse, values):
    return product(stacked(values), split(inverse), ROWS_OUT)


def gather_row(vert_ref, index):
    tiles = vert_ref.shape[1] // LANES
    lane, tile = index % LANES, index // LANES
    found = []
    for axis in range(3):
        total = jnp.zeros(index.shape, jnp.float32)
        for at in range(tiles):
            table = jnp.broadcast_to(vert_ref[axis : axis + 1, at * LANES : (at + 1) * LANES], index.shape)
            total = jnp.where(tile == at, jnp.take_along_axis(table, lane, axis=1), total)
        found.append(total)
    return found


def first_kernel(couple, core_ref, pos_ref, vert_ref, conn_ref, erhs_ref, drhs_ref, einv_ref, dinv_ref,
                 high_ref, low_ref, elec_ref, keep_ref, send_ref, place, centre, wide, held_d, both_d, field):
    elec, drop = high_ref.shape
    rows = erhs_ref.shape[0]
    half = drop // 2
    half_block = vert_ref.shape[1]
    for at in range(drop // LANES):
        cols = slice(at * LANES, (at + 1) * LANES)
        corners = gather_row(vert_ref, conn_ref[:, cols] % half_block)
        for axis in range(3):
            g = corners[axis]
            centre[axis : axis + 1, cols] = (g[0:1] + g[1:2] + g[2:3]) / 3.0
    place[...] = jnp.zeros_like(place)
    place[0:3, :] = pos_ref[...]
    upright = place[...].T
    for axis in range(3):
        wide[axis] = jnp.broadcast_to(upright[:, axis : axis + 1], (elec, LANES))
    pieces = []
    for at in range(elec // LANES):
        pieces.append(solve_block(einv_ref[at], erhs_ref[:, at * LANES : (at + 1) * LANES]))
    charge_elec = stacked(jnp.concatenate(pieces, axis=1))
    for at in range(drop // LANES):
        cols = slice(at * LANES, (at + 1) * LANES)
        solved = solve_block(dinv_ref[at], drhs_ref[:, cols])
        high, both = stacked(solved)
        both_d[:, cols] = both
    total = jnp.zeros((rows, elec), jnp.float32)
    for at in range(drop // CHUNK):
        cols = slice(at * CHUNK, (at + 1) * CHUNK)
        tiles = []
        for lane in range(at * CHUNK, (at + 1) * CHUNK, LANES):
            here = slice(lane, lane + LANES)
            dx = wide[0] - centre[0:1, here]
            dy = wide[1] - centre[1:2, here]
            dz = wide[2] - centre[2:3, here]
            square = dx * dx + dy * dy + dz * dz + SOFTEN
            inverse = lax.rsqrt(square)
            tiles.append(jnp.exp((square * inverse) * -SCREEN) * inverse)
        weights = split(jnp.concatenate(tiles, axis=1))
        high_ref[:, cols], low_ref[:, cols] = weights
        both = both_d[:, cols]
        total = total + product((both[:rows], both), weights, ROWS_OUT)
        field[:, cols] = product(charge_elec, weights, ROWS_IN) * couple
    elec_ref[...] = total * couple
    mine = pl.multiple_of(core_ref[0] * half, half)
    other = pl.multiple_of((1 - core_ref[0]) * half, half)
    keep_ref[...] = field[:, pl.ds(mine, half)]
    send_ref[...] = field[:, pl.ds(other, half)]


def first(core, couple, elec_pos, drop_vert, drop_conn, elec_rhs, drop_rhs, elec_inv, drop_inv):
    rows, elec = elec_rhs.shape
    drop = drop_rhs.shape[1]
    return pl.pallas_call(
        lambda *refs: first_kernel(couple, *refs),
        out_shape=[
            jax.ShapeDtypeStruct((elec, drop), jnp.bfloat16),
            jax.ShapeDtypeStruct((elec, drop), jnp.bfloat16),
            jax.ShapeDtypeStruct((rows, elec), jnp.float32),
            jax.ShapeDtypeStruct((rows, drop // 2), jnp.float32),
            jax.ShapeDtypeStruct((rows, drop // 2), jnp.float32),
        ],
        in_specs=[SMEM] + [VMEM] * 7,
        out_specs=[VMEM] * 5,
        scratch_shapes=[
            pltpu.VMEM((LANES, elec), jnp.float32),
            pltpu.VMEM((8, drop), jnp.float32),
            pltpu.VMEM((3, elec, LANES), jnp.float32),
            pltpu.VMEM((8, LANES), jnp.float32),
            pltpu.VMEM((2 * rows, drop), jnp.bfloat16),
            pltpu.VMEM((rows, drop), jnp.float32),
        ],
        compiler_params=PARAMS,
        name="coupling_and_first_fields",
    )(core, elec_pos, drop_vert, drop_conn, elec_rhs, drop_rhs, elec_inv, drop_inv)


def drop_solve_kernel(core_ref, rhs_ref, inv_ref, left_ref, right_ref, out_ref):
    for at in range(out_ref.shape[1] // LANES):
        cols = slice(at * LANES, (at + 1) * LANES)
        out_ref[:, cols] = solve_block(inv_ref[at], rhs_ref[:, cols] - (left_ref[:, cols] + right_ref[:, cols]))


def drop_solve(core, drop_rhs, drop_inv, left, right):
    rows, half = left.shape
    whole = pl.BlockSpec((rows, half), lambda i, core: (0, 0))
    return pl.pallas_call(
        drop_solve_kernel,
        out_shape=jax.ShapeDtypeStruct((rows, half), jnp.float32),
        grid_spec=pltpu.PrefetchScalarGridSpec(
            num_scalar_prefetch=1,
            grid=(1,),
            in_specs=[
                pl.BlockSpec((rows, half), lambda i, core: (0, core[0])),
                pl.BlockSpec((half // LANES, LANES, LANES), lambda i, core: (core[0], 0, 0)),
                whole,
                whole,
            ],
            out_specs=whole,
        ),
        compiler_params=PARAMS,
        name="drop_charges",
    )(core, drop_rhs, drop_inv, left, right)


def elec_charge(rhs_ref, inv_ref, left_ref, right_ref):
    pieces = []
    for at in range(rhs_ref.shape[1] // LANES):
        cols = slice(at * LANES, (at + 1) * LANES)
        pieces.append(solve_block(inv_ref[at], rhs_ref[:, cols] - (left_ref[:, cols] + right_ref[:, cols])))
    return jnp.concatenate(pieces, axis=1)


def elec_solve_kernel(rhs_ref, inv_ref, left_ref, right_ref, out_ref):
    out_ref[...] = elec_charge(rhs_ref, inv_ref, left_ref, right_ref)


def elec_solve(elec_rhs, elec_inv, left, right):
    return pl.pallas_call(
        elec_solve_kernel,
        out_shape=jax.ShapeDtypeStruct(left.shape, jnp.float32),
        in_specs=[VMEM] * 4,
        out_specs=VMEM,
        compiler_params=PARAMS,
        name="elec_charges",
    )(elec_rhs, elec_inv, left, right)


def to_drop_kernel(couple, core_ref, rhs_ref, inv_ref, left_ref, right_ref, high_ref, low_ref, keep_ref, send_ref):
    half = keep_ref.shape[1]
    charge = stacked(elec_charge(rhs_ref, inv_ref, left_ref, right_ref))
    for place, out_ref in ((1 - core_ref[0], send_ref), (core_ref[0], keep_ref)):
        for at in range(half // CHUNK):
            cols = pl.ds(pl.multiple_of(place * half + at * CHUNK, CHUNK), CHUNK)
            here = slice(at * CHUNK, (at + 1) * CHUNK)
            out_ref[:, here] = product(charge, (high_ref[:, cols], low_ref[:, cols]), ROWS_IN) * couple


def to_drop(core, couple, elec_rhs, elec_inv, left, right, high, low):
    rows = elec_rhs.shape[0]
    half = high.shape[1] // 2
    return pl.pallas_call(
        lambda *refs: to_drop_kernel(couple, *refs),
        out_shape=[jax.ShapeDtypeStruct((rows, half), jnp.float32)] * 2,
        in_specs=[SMEM] + [VMEM] * 6,
        out_specs=[VMEM] * 2,
        compiler_params=PARAMS,
        name="elec_charges_to_drop_field",
    )(core, elec_rhs, elec_inv, left, right, high, low)


def to_elec_kernel(couple, core_ref, own_ref, other_ref, high_ref, low_ref, out_ref):
    half = own_ref.shape[1]
    total = jnp.zeros(out_ref.shape, jnp.float32)
    for place, charge_ref in ((core_ref[0], own_ref), (1 - core_ref[0], other_ref)):
        for at in range(half // CHUNK):
            cols = pl.ds(pl.multiple_of(place * half + at * CHUNK, CHUNK), CHUNK)
            here = slice(at * CHUNK, (at + 1) * CHUNK)
            total = total + product(stacked(charge_ref[:, here]), (high_ref[:, cols], low_ref[:, cols]), ROWS_OUT)
    out_ref[...] = total * couple


def to_elec(core, couple, own, other, high, low):
    return pl.pallas_call(
        lambda *refs: to_elec_kernel(couple, *refs),
        out_shape=jax.ShapeDtypeStruct((own.shape[0], high.shape[0]), jnp.float32),
        in_specs=[SMEM] + [VMEM] * 4,
        out_specs=VMEM,
        compiler_params=PARAMS,
        name="drop_charges_to_elec_field",
    )(core, own, other, high, low)


def join_kernel(core_ref, own_ref, other_ref, out_ref):
    half = own_ref.shape[1]
    out_ref[:, pl.ds(pl.multiple_of(core_ref[0] * half, half), half)] = own_ref[...]
    out_ref[:, pl.ds(pl.multiple_of((1 - core_ref[0]) * half, half), half)] = other_ref[...]


def join(core, own, other):
    rows, half = own.shape
    return pl.pallas_call(
        join_kernel,
        out_shape=jax.ShapeDtypeStruct((rows, 2 * half), jnp.float32),
        in_specs=[SMEM] + [VMEM] * 2,
        out_specs=VMEM,
        compiler_params=PARAMS,
        name="join_halves",
    )(core, own, other)


def exchanges(elec_devices, drop_devices):
    def pairs(partner):
        out = []
        for elec in range(elec_devices):
            for drop in range(drop_devices):
                to_elec, to_drop = partner(elec, drop)
                out.append((elec * drop_devices + drop, to_elec * drop_devices + to_drop))
        return out

    def ordered(bits, step, core):
        return bits[step] if core == 0 else bits[len(bits) - 1 - step]

    chip_bits = range(1, elec_devices.bit_length() - 1)
    drop_bits = range(drop_devices.bit_length() - 1)
    core = pairs(lambda e, d: (e ^ 1, d))
    plane = [
        pairs(lambda e, d, s=s: (e ^ (1 << ordered(chip_bits, s, e & 1)), d)) for s in range(len(chip_bits))
    ]
    line = [
        pairs(lambda e, d, s=s: (e, d ^ (1 << ordered(drop_bits, s, e & 1)))) for s in range(len(drop_bits))
    ]
    return core, plane, line


def solution(mesh):
    elec_devices, drop_devices = mesh.shape["elec"], mesh.shape["drop"]
    core_pairs, plane_pairs, line_pairs = exchanges(elec_devices, drop_devices)

    def swap(value, pairs):
        return lax.ppermute(value, ("elec", "drop"), pairs)

    def summed(value, steps):
        for pairs in steps[:-1]:
            value = value + swap(value, pairs)
        return value, swap(value, steps[-1])

    def on_device(elec_pos, drop_vert, drop_conn, elec_rhs, drop_rhs, elec_inv, drop_inv):
        couple = couple_of(drop_rhs.shape[1] * drop_devices)
        core = (lax.axis_index("elec") % 2).astype(jnp.int32).reshape(1)
        high, low, elec_1, keep_1, send_1 = first(
            core, couple, elec_pos, drop_vert, drop_conn, elec_rhs, drop_rhs, elec_inv, drop_inv
        )
        drop_1 = summed(keep_1 + swap(send_1, core_pairs), plane_pairs)
        elec_1 = summed(elec_1, line_pairs)
        keep_2, send_2 = to_drop(core, couple, elec_rhs, elec_inv, *elec_1, high, low)
        own_1 = drop_solve(core, drop_rhs, drop_inv, *drop_1)
        other_1 = swap(own_1, core_pairs)
        elec_2 = to_elec(core, couple, own_1, other_1, high, low)
        drop_2 = summed(keep_2 + swap(send_2, core_pairs), plane_pairs)
        elec_2 = summed(elec_2, line_pairs)
        own_2 = drop_solve(core, drop_rhs, drop_inv, *drop_2)
        charge_drop = join(core, own_2, swap(own_2, core_pairs))
        charge_elec = elec_solve(elec_rhs, elec_inv, *elec_2)
        return (charge_elec, charge_drop)

    placed = (
        P(None, "elec"),
        P(None, "drop"),
        P(None, "drop"),
        P(None, "elec"),
        P(None, "drop"),
        P("elec", None, None),
        P("drop", None, None),
    )
    return jax.shard_map(
        on_device,
        mesh=mesh,
        in_specs=placed,
        out_specs=(P(None, "elec"), P(None, "drop")),
        check_vma=False,
    )
```

```python
import functools
import math

import jax
import jax.numpy as jnp
from jax import lax
from jax.experimental import pallas as pl
from jax.experimental.pallas import tpu as pltpu
from jax.sharding import PartitionSpec as P

SOFTEN = 0.001
SCREEN = 1.0
LANES = 128
CHUNK = 256
VMEM = pl.BlockSpec(memory_space=pltpu.VMEM)
SMEM = pl.BlockSpec(memory_space=pltpu.SMEM)
HBM = pl.BlockSpec(memory_space=pltpu.HBM)
ROWS_IN = ((1,), (0,))
ROWS_OUT = ((1,), (1,))


def couple_of(total_drop):
    return 1.0 / (3.0 * math.sqrt(total_drop))


def split(value):
    high = value.astype(jnp.bfloat16)
    low = (value - high.astype(jnp.float32)).astype(jnp.bfloat16)
    return high, low


def stacked(value):
    return jnp.concatenate(split(value), axis=0)


def product(both, weights, contract):
    weight_high, weight_low = weights
    rows = both.shape[0] // 2
    dims = (contract, ((), ()))
    first = lax.dot_general(both, weight_high, dims, preferred_element_type=jnp.float32)
    second = lax.dot_general(both[:rows], weight_low, dims, preferred_element_type=jnp.float32)
    return first[:rows] + (first[rows:] + second)


def solve_block(inverse, values):
    return product(stacked(values), split(inverse), ROWS_OUT)


def solve(inv_ref, values):
    pieces = []
    for at in range(values.shape[1] // LANES):
        pieces.append(solve_block(inv_ref[at], values[:, at * LANES : (at + 1) * LANES]))
    return jnp.concatenate(pieces, axis=1)


def gather(vert_ref, index):
    lane, tile = index % LANES, index // LANES
    found = []
    for axis in range(3):
        total = jnp.zeros(index.shape, jnp.float32)
        for at in range(vert_ref.shape[1] // LANES):
            table = jnp.broadcast_to(vert_ref[axis : axis + 1, at * LANES : (at + 1) * LANES], index.shape)
            total = jnp.where(tile == at, jnp.take_along_axis(table, lane, axis=1), total)
        found.append(total)
    return found


def fill_centres(vert_ref, conn_ref, centre):
    half_block = vert_ref.shape[1]
    for at in range(conn_ref.shape[1] // LANES):
        cols = slice(at * LANES, (at + 1) * LANES)
        corners = gather(vert_ref, conn_ref[:, cols] % half_block)
        for axis in range(3):
            g = corners[axis]
            centre[axis : axis + 1, cols] = (g[0:1] + g[1:2] + g[2:3]) / 3.0


def coupling_chunk(wide, centre, start):
    tiles = []
    for lane in range(start, start + CHUNK, LANES):
        here = slice(lane, lane + LANES)
        dx = wide[0] - centre[0:1, here]
        dy = wide[1] - centre[1:2, here]
        dz = wide[2] - centre[2:3, here]
        square = dx * dx + dy * dy + dz * dz + SOFTEN
        inverse = lax.rsqrt(square)
        tiles.append(jnp.exp((square * inverse) * -SCREEN) * inverse)
    return split(jnp.concatenate(tiles, axis=1))


def columns(place, width):
    return pl.ds(pl.multiple_of(place * width, width), width)


def first_kernel(couple, core_ref, pos_hbm, vert_hbm, conn_hbm, erhs_hbm, einv_hbm, drhs_hbm, dinv_hbm,
                 ohigh_ref, olow_ref, high_ref, low_ref, send_ref, keep_ref, elec_ref, erhs, einv, drhs, dinv,
                 pos, vert, conn, place, wide, centre, sems):
    elec, half = high_ref.shape
    blocks = half // LANES
    moves = ((conn_hbm, conn), (vert_hbm, vert), (pos_hbm, pos), (erhs_hbm, erhs), (einv_hbm, einv),
             (drhs_hbm, drhs), (dinv_hbm, dinv))
    copies = [pltpu.make_async_copy(here, there, sems.at[at]) for at, (here, there) in enumerate(moves)]
    for copy in copies:
        copy.start()
    for copy in copies[:3]:
        copy.wait()
    place[...] = jnp.zeros_like(place)
    place[0:3, :] = pos[...]
    upright = place[...].T
    for axis in range(3):
        wide[axis] = jnp.broadcast_to(upright[:, axis : axis + 1], (elec, LANES))
    fill_centres(vert, conn, centre)
    for copy in copies[3:]:
        copy.wait()
    both = stacked(solve(einv, erhs[...]))
    total = jnp.zeros(elec_ref.shape, jnp.float32)
    for place_at, parts, field_ref in (
        (1 - core_ref[0], (ohigh_ref, olow_ref), send_ref),
        (core_ref[0], (high_ref, low_ref), keep_ref),
    ):
        here = columns(place_at, half)
        centres = centre[:, here]
        charge = stacked(solve(dinv.at[pl.ds(place_at * blocks, blocks)], drhs[:, here]))
        for start in range(0, half, CHUNK):
            cols = slice(start, start + CHUNK)
            weights = coupling_chunk(wide, centres, start)
            parts[0][:, cols], parts[1][:, cols] = weights
            field_ref[:, cols] = product(both, weights, ROWS_IN) * couple
            total = total + product(charge[:, cols], weights, ROWS_OUT)
    elec_ref[...] = total * couple


def add_pairs_kernel(a_ref, b_ref, c_ref, d_ref, ab_ref, cd_ref):
    ab_ref[...] = a_ref[...] + b_ref[...]
    cd_ref[...] = c_ref[...] + d_ref[...]


def to_drop_kernel(couple, rhs_ref, inv_ref, field_ref, high_ref, low_ref, send_ref, both_ref):
    both = stacked(solve(inv_ref, rhs_ref[...] - field_ref[...]))
    both_ref[...] = both
    for start in range(0, high_ref.shape[1], CHUNK):
        cols = slice(start, start + CHUNK)
        send_ref[:, cols] = product(both, (high_ref[:, cols], low_ref[:, cols]), ROWS_IN) * couple


def halves_kernel(couple, core_ref, both_ref, rhs_ref, inv_ref, field_ref, high_ref, low_ref, keep_ref, elec_ref):
    half = high_ref.shape[1]
    blocks = half // LANES
    keep_ref[...] = product(both_ref[...], (high_ref[...], low_ref[...]), ROWS_IN) * couple
    values = rhs_ref[:, columns(core_ref[0], half)] - field_ref[...]
    charge = solve(inv_ref.at[pl.ds(core_ref[0] * blocks, blocks)], values)
    elec_ref[...] = product(stacked(charge), (high_ref[...], low_ref[...]), ROWS_OUT)


def to_elec_kernel(couple, core_ref, rhs_ref, inv_ref, field_ref, part_ref, high_ref, low_ref, keep_ref, send_ref,
                   elec_ref, sum_ref):
    half = high_ref.shape[1]
    blocks = half // LANES
    other = 1 - core_ref[0]
    sum_ref[...] = keep_ref[...] + send_ref[...]
    values = rhs_ref[:, columns(other, half)] - field_ref[...]
    charge = solve(inv_ref.at[pl.ds(other * blocks, blocks)], values)
    elec_ref[...] = (part_ref[...] + product(stacked(charge), (high_ref[...], low_ref[...]), ROWS_OUT)) * couple


def elec_kernel(rhs_ref, inv_ref, field_ref, out_ref):
    out_ref[...] = solve(inv_ref, rhs_ref[...] - field_ref[...])


def drop_kernel(core_ref, rhs_ref, inv_ref, own_ref, other_ref, out_ref):
    half = own_ref.shape[1]
    blocks = half // LANES
    for place, field_ref in ((core_ref[0], own_ref), (1 - core_ref[0], other_ref)):
        cols = columns(place, half)
        out_ref[:, cols] = solve(inv_ref.at[pl.ds(place * blocks, blocks)], rhs_ref[:, cols] - field_ref[...])


def run(kernel, name, micros, operands, specs, outs, scratch=()):
    return pl.pallas_call(
        kernel,
        out_shape=[jax.ShapeDtypeStruct(shape, dtype) for shape, dtype in outs],
        in_specs=specs,
        out_specs=[VMEM] * len(outs),
        scratch_shapes=list(scratch),
        compiler_params=pltpu.CompilerParams(vmem_limit_bytes=32 * 2**20),
        cost_estimate=pl.CostEstimate(flops=0, bytes_accessed=int(micros * 3.3e6), transcendentals=0),
        name=name,
    )(*operands)


def exchanges(elec_devices, drop_devices):
    def pairs(partner):
        out = []
        for elec in range(elec_devices):
            for drop in range(drop_devices):
                to_elec, to_drop = partner(elec, drop)
                out.append((elec * drop_devices + drop, to_elec * drop_devices + to_drop))
        return out

    def ordered(bits, step, core):
        return bits[step] if core == 0 else bits[len(bits) - 1 - step]

    chip_bits = range(1, elec_devices.bit_length() - 1)
    drop_bits = range(drop_devices.bit_length() - 1)
    core = pairs(lambda e, d: (e ^ 1, d))
    plane = [
        pairs(lambda e, d, s=s: (e ^ (1 << ordered(chip_bits, s, e & 1)), d)) for s in range(len(chip_bits))
    ]
    line = [
        pairs(lambda e, d, s=s: (e, d ^ (1 << ordered(drop_bits, s, e & 1)))) for s in range(len(drop_bits))
    ]
    return core, plane, line


def solution(mesh):
    elec_devices, drop_devices = mesh.shape["elec"], mesh.shape["drop"]
    core_pairs, plane_pairs, line_pairs = exchanges(elec_devices, drop_devices)

    def swap(value, pairs):
        return lax.ppermute(value, ("elec", "drop"), pairs)

    def sums(line, plane):
        for at in range(max(len(line_pairs), len(plane_pairs))):
            line_got = swap(line, line_pairs[at]) if at < len(line_pairs) else jnp.zeros_like(line)
            plane_got = swap(plane, plane_pairs[at]) if at < len(plane_pairs) else jnp.zeros_like(plane)
            line, plane = run(
                add_pairs_kernel, "add_pairs", 0.1,
                (line, line_got, plane, plane_got),
                [VMEM] * 4,
                [(line.shape, jnp.float32), (plane.shape, jnp.float32)],
            )
        return line, plane

    def on_device(elec_pos, drop_vert, drop_conn, elec_rhs, drop_rhs, elec_inv, drop_inv):
        f32, bf16 = jnp.float32, jnp.bfloat16
        rows, elec = elec_rhs.shape
        drop = drop_rhs.shape[1]
        half = drop // 2
        couple = couple_of(drop * drop_devices)
        core = (lax.axis_index("elec") % 2).astype(jnp.int32).reshape(1)

        inputs = (elec_pos, drop_vert, drop_conn, elec_rhs, elec_inv, drop_rhs, drop_inv)
        outs = [((elec, half), bf16)] * 4 + [((rows, half), f32)] * 2 + [((rows, elec), f32)]
        outs += [(value.shape, f32) for value in inputs[3:]]
        other_high, other_low, own_high, own_low, send, keep, line, elec_rhs, elec_inv, drop_rhs, drop_inv = run(
            functools.partial(first_kernel, couple), "coupling_and_first_fields", 5.0,
            (core, *(pltpu.with_memory_space_constraint(value, pltpu.HBM) for value in inputs)),
            [SMEM] + [HBM] * 7,
            outs,
            [pltpu.VMEM(value.shape, value.dtype) for value in inputs[:3]]
            + [pltpu.VMEM((LANES, elec), f32), pltpu.VMEM((3, elec, LANES), f32), pltpu.VMEM((8, drop), f32),
               pltpu.SemaphoreType.DMA((7,))],
        )
        got = swap(send, core_pairs)
        line, plane = sums(line, keep + got)

        plane_got = swap(plane, core_pairs)
        send, both = run(
            functools.partial(to_drop_kernel, couple), "elec_charges_to_drop_field", 0.8,
            (elec_rhs, elec_inv, line, other_high, other_low),
            [VMEM] * 5,
            [((rows, half), f32), ((2 * rows, elec), bf16)],
        )
        got = swap(send, core_pairs)
        keep, part = run(
            functools.partial(halves_kernel, couple), "fields_of_own_half", 2.0,
            (core, both, drop_rhs, drop_inv, plane, own_high, own_low),
            [SMEM] + [VMEM] * 6,
            [((rows, half), f32), ((rows, elec), f32)],
        )
        line, plane = run(
            functools.partial(to_elec_kernel, couple), "field_of_other_half", 1.4,
            (core, drop_rhs, drop_inv, plane_got, part, other_high, other_low, keep, got),
            [SMEM] + [VMEM] * 8,
            [((rows, elec), f32), ((rows, half), f32)],
        )
        line, plane = sums(line, plane)

        plane_got = swap(plane, core_pairs)
        charge_elec, = run(
            elec_kernel, "elec_charges", 1.0, (elec_rhs, elec_inv, line), [VMEM] * 3, [((rows, elec), f32)]
        )
        charge_drop, = run(
            drop_kernel, "drop_charges", 1.8, (core, drop_rhs, drop_inv, plane, plane_got), [SMEM] + [VMEM] * 4,
            [((rows, drop), f32)],
        )
        return (charge_elec, charge_drop)

    placed = (
        P(None, "elec"),
        P(None, "drop"),
        P(None, "drop"),
        P(None, "elec"),
        P(None, "drop"),
        P("elec", None, None),
        P("drop", None, None),
    )
    return jax.shard_map(
        on_device,
        mesh=mesh,
        in_specs=placed,
        out_specs=(P(None, "elec"), P(None, "drop")),
        check_vma=False,
    )
```

```python
import functools
import math

import jax
import jax.numpy as jnp
from jax import lax
from jax.experimental import pallas as pl
from jax.experimental.pallas import tpu as pltpu
from jax.sharding import PartitionSpec as P

SOFTEN = 0.001
SCREEN = 1.0
LANES = 128
CHUNK = 256
VMEM = pl.BlockSpec(memory_space=pltpu.VMEM)
SMEM = pl.BlockSpec(memory_space=pltpu.SMEM)
ANY = pl.BlockSpec(memory_space=pl.ANY)
HBM = pl.BlockSpec(memory_space=pltpu.HBM)
ROWS_IN = ((1,), (0,))
ROWS_OUT = ((1,), (1,))


def couple_of(total_drop):
    return 1.0 / (3.0 * math.sqrt(total_drop))


def split(value):
    high = value.astype(jnp.bfloat16)
    low = (value - high.astype(jnp.float32)).astype(jnp.bfloat16)
    return high, low


def stacked(value):
    return jnp.concatenate(split(value), axis=0)


def product(both, weights, contract):
    weight_high, weight_low = weights
    rows = both.shape[0] // 2
    dims = (contract, ((), ()))
    first = lax.dot_general(both, weight_high, dims, preferred_element_type=jnp.float32)
    second = lax.dot_general(both[:rows], weight_low, dims, preferred_element_type=jnp.float32)
    return first[:rows] + (first[rows:] + second)


def solve_block(inverse, values):
    return product(stacked(values), split(inverse), ROWS_OUT)


def solve(inv_ref, values):
    pieces = []
    for at in range(values.shape[1] // LANES):
        pieces.append(solve_block(inv_ref[at], values[:, at * LANES : (at + 1) * LANES]))
    return jnp.concatenate(pieces, axis=1)


def gather(vert_ref, index):
    lane, tile = index % LANES, index // LANES
    found = []
    for axis in range(3):
        total = jnp.zeros(index.shape, jnp.float32)
        for at in range(vert_ref.shape[1] // LANES):
            table = jnp.broadcast_to(vert_ref[axis : axis + 1, at * LANES : (at + 1) * LANES], index.shape)
            total = jnp.where(tile == at, jnp.take_along_axis(table, lane, axis=1), total)
        found.append(total)
    return found


def fill_centres(vert_ref, conn_ref, centre):
    half_block = vert_ref.shape[1]
    for at in range(conn_ref.shape[1] // LANES):
        cols = slice(at * LANES, (at + 1) * LANES)
        corners = gather(vert_ref, conn_ref[:, cols] % half_block)
        for axis in range(3):
            g = corners[axis]
            centre[axis : axis + 1, cols] = (g[0:1] + g[1:2] + g[2:3]) / 3.0


def coupling_chunk(wide, centre, start):
    tiles = []
    for lane in range(start, start + CHUNK, LANES):
        here = slice(lane, lane + LANES)
        dx = wide[0] - centre[0:1, here]
        dy = wide[1] - centre[1:2, here]
        dz = wide[2] - centre[2:3, here]
        square = dx * dx + dy * dy + dz * dz + SOFTEN
        inverse = lax.rsqrt(square)
        tiles.append(jnp.exp((square * inverse) * -SCREEN) * inverse)
    return split(jnp.concatenate(tiles, axis=1))


def columns(place, width):
    return pl.ds(pl.multiple_of(place * width, width), width)


def spread(pos, wide):
    upright = jnp.concatenate([pos, jnp.zeros((LANES - pos.shape[0], pos.shape[1]), jnp.float32)], axis=0).T
    for axis in range(3):
        wide[axis] = jnp.broadcast_to(upright[:, axis : axis + 1], (pos.shape[1], LANES))


def first_kernel(couple, core_ref, pos_hbm, vert_hbm, conn_hbm, erhs_hbm, einv_hbm, drhs_hbm, dinv_hbm,
                 high_ref, low_ref, send_ref, wide_ref, centre_ref, elec_ref, own_ref, other_ref,
                 erhs, einv, drhs, dinv, pos, vert, conn, centre, sems):
    half = high_ref.shape[1]
    blocks = half // LANES
    moves = ((conn_hbm, conn), (vert_hbm, vert), (pos_hbm, pos), (erhs_hbm, erhs), (einv_hbm, einv),
             (drhs_hbm, drhs), (dinv_hbm, dinv))
    copies = [pltpu.make_async_copy(here, there, sems.at[at]) for at, (here, there) in enumerate(moves)]
    for copy in copies:
        copy.start()
    for copy in copies[:3]:
        copy.wait()
    spread(pos[...], wide_ref)
    fill_centres(vert, conn, centre)
    for copy in copies[3:]:
        copy.wait()
    both = stacked(solve(einv, erhs[...]))
    elec_ref[...] = both
    own, other = core_ref[0], 1 - core_ref[0]
    centre_ref[...] = centre[:, columns(own, half)]
    centres = centre[:, columns(other, half)]
    for start in range(0, half, CHUNK):
        cols = slice(start, start + CHUNK)
        weights = coupling_chunk(wide_ref, centres, start)
        high_ref[:, cols], low_ref[:, cols] = weights
        send_ref[:, cols] = product(both, weights, ROWS_IN) * couple
        for place, out_ref in ((own, own_ref), (other, other_ref)):
            block = place * blocks + start // LANES
            here = pl.ds(pl.multiple_of(place * half + start, CHUNK), CHUNK)
            out_ref[:, cols] = stacked(solve(dinv.at[pl.ds(block, CHUNK // LANES)], drhs[:, here]))


def second_kernel(couple, wide_ref, centre_ref, both_ref, own_ref, other_ref, ohigh_ref, olow_ref,
                  high_ref, low_ref, keep_ref, elec_ref):
    total = jnp.zeros(elec_ref.shape, jnp.float32)
    for start in range(0, high_ref.shape[1], CHUNK):
        cols = slice(start, start + CHUNK)
        weights = coupling_chunk(wide_ref, centre_ref, start)
        high_ref[:, cols], low_ref[:, cols] = weights
        keep_ref[:, cols] = product(both_ref[...], weights, ROWS_IN) * couple
        total = total + product(other_ref[:, cols], (ohigh_ref[:, cols], olow_ref[:, cols]), ROWS_OUT)
        total = total + product(own_ref[:, cols], weights, ROWS_OUT)
    elec_ref[...] = total * couple


def drop_charge(place, rhs_ref, inv_ref, field):
    half = field.shape[1]
    blocks = half // LANES
    return solve(inv_ref.at[pl.ds(place * blocks, blocks)], rhs_ref[:, columns(place, half)] - field)


def add_kernel(a_ref, b_ref, *rest):
    rest[-1][...] = a_ref[...] + b_ref[...]


def add_pairs_kernel(a_ref, b_ref, c_ref, d_ref, ab_ref, cd_ref):
    ab_ref[...] = a_ref[...] + b_ref[...]
    cd_ref[...] = c_ref[...] + d_ref[...]


def middle_kernel(couple, line_ref, line_got_ref, plane_ref, plane_got_ref, rhs_ref, inv_ref, high_ref, low_ref,
                  two_ref, both_ref):
    two_ref[0] = plane_ref[...] + plane_got_ref[...]
    both = stacked(solve(inv_ref, rhs_ref[...] - (line_ref[...] + line_got_ref[...])))
    both_ref[...] = both
    two_ref[1] = product(both, (high_ref[...], low_ref[...]), ROWS_IN) * couple


def own_kernel(couple, core_ref, both_ref, rhs_ref, inv_ref, two_ref, high_ref, low_ref, keep_ref, elec_ref):
    weights = high_ref[...], low_ref[...]
    keep_ref[...] = product(both_ref[...], weights, ROWS_IN) * couple
    charge = drop_charge(core_ref[0], rhs_ref, inv_ref, two_ref[0])
    elec_ref[...] = product(stacked(charge), weights, ROWS_OUT)


def plane_kernel(keep_ref, two_ref, out_ref):
    out_ref[...] = keep_ref[...] + two_ref[1]


def other_kernel(couple, core_ref, rhs_ref, inv_ref, two_ref, share_ref, high_ref, low_ref, elec_ref):
    charge = drop_charge(1 - core_ref[0], rhs_ref, inv_ref, two_ref[0])
    elec_ref[...] = (share_ref[...] + product(stacked(charge), (high_ref[...], low_ref[...]), ROWS_OUT)) * couple


def charges_kernel(core_ref, erhs_ref, einv_ref, line_ref, drhs_ref, dinv_ref, plane_ref, elec_hbm, drop_hbm,
                   elec, half, sems):
    elec[...] = solve(einv_ref, erhs_ref[...] - line_ref[...])
    elec_copy = pltpu.make_async_copy(elec, elec_hbm, sems.at[0])
    elec_copy.start()
    half[...] = drop_charge(core_ref[0], drhs_ref, dinv_ref, plane_ref[...])
    drop_copy = pltpu.make_async_copy(half, drop_hbm.at[:, columns(core_ref[0], half.shape[1])], sems.at[1])
    drop_copy.start()
    elec_copy.wait()
    drop_copy.wait()


def rest_kernel(core_ref, rhs_ref, inv_ref, field_ref, _, drop_hbm, half, sems):
    width = half.shape[1] // 2
    blocks = width // LANES
    copies = []
    for at in range(2):
        place = (1 - core_ref[0]) * 2 + at
        here = slice(at * width, (at + 1) * width)
        values = rhs_ref[:, columns(place, width)] - field_ref[:, here]
        half[:, here] = solve(inv_ref.at[pl.ds(place * blocks, blocks)], values)
        copies.append(pltpu.make_async_copy(half.at[:, here], drop_hbm.at[:, columns(place, width)], sems.at[at]))
        copies[-1].start()
    for copy in copies:
        copy.wait()


def run(kernel, name, micros, operands, specs, outs, scratch=(), out_spec=VMEM, aliases=()):
    return pl.pallas_call(
        kernel,
        out_shape=[jax.ShapeDtypeStruct(shape, dtype) for shape, dtype in outs],
        in_specs=specs,
        out_specs=[out_spec] * len(outs),
        input_output_aliases=dict(aliases),
        scratch_shapes=list(scratch),
        compiler_params=pltpu.CompilerParams(vmem_limit_bytes=32 * 2**20),
        cost_estimate=pl.CostEstimate(flops=0, bytes_accessed=int(micros * 3.3e6), transcendentals=0),
        name=name,
    )(*operands)


def add(left, right, *after):
    return run(
        add_kernel, "add", 0.1, (left, right, *after), [VMEM] * 2 + [ANY] * len(after), [(left.shape, jnp.float32)]
    )[0]


def exchanges(elec_devices, drop_devices):
    def pairs(partner):
        out = []
        for elec in range(elec_devices):
            for drop in range(drop_devices):
                to_elec, to_drop = partner(elec, drop)
                out.append((elec * drop_devices + drop, to_elec * drop_devices + to_drop))
        return out

    def ordered(bits, step, core):
        return bits[step] if core == 0 else bits[len(bits) - 1 - step]

    chip_bits = range(1, elec_devices.bit_length() - 1)
    drop_bits = range(drop_devices.bit_length() - 1)
    core = pairs(lambda e, d: (e ^ 1, d))
    plane = [
        pairs(lambda e, d, s=s: (e ^ (1 << ordered(chip_bits, s, e & 1)), d)) for s in range(len(chip_bits))
    ]
    line = [
        pairs(lambda e, d, s=s: (e, d ^ (1 << ordered(drop_bits, s, e & 1)))) for s in range(len(drop_bits))
    ]
    return core, plane, line


def solution(mesh):
    elec_devices, drop_devices = mesh.shape["elec"], mesh.shape["drop"]
    core_pairs, plane_pairs, line_pairs = exchanges(elec_devices, drop_devices)

    def swap(value, pairs):
        return lax.ppermute(value, ("elec", "drop"), pairs)

    def sums(line, plane):
        for at in range(max(len(line_pairs), len(plane_pairs)) - 1):
            line_got = swap(line, line_pairs[at]) if at < len(line_pairs) - 1 else jnp.zeros_like(line)
            plane_got = swap(plane, plane_pairs[at]) if at < len(plane_pairs) - 1 else jnp.zeros_like(plane)
            plane = add(plane, plane_got)
            line = add(line, line_got, plane)
        return line, swap(line, line_pairs[-1]), plane, swap(plane, plane_pairs[-1])

    def on_device(elec_pos, drop_vert, drop_conn, elec_rhs, drop_rhs, elec_inv, drop_inv):
        f32, bf16 = jnp.float32, jnp.bfloat16
        rows, elec = elec_rhs.shape
        drop = drop_rhs.shape[1]
        half = drop // 2
        couple = couple_of(drop * drop_devices)
        core = (lax.axis_index("elec") % 2).astype(jnp.int32).reshape(1)

        inputs = (elec_pos, drop_vert, drop_conn, elec_rhs, elec_inv, drop_rhs, drop_inv)
        outs = [((elec, half), bf16)] * 2 + [((rows, half), f32), ((3, elec, LANES), f32), ((8, half), f32)]
        outs += [((2 * rows, elec), bf16)] + [((2 * rows, half), bf16)] * 2 + [(value.shape, f32) for value in inputs[3:]]
        (other_high, other_low, send, wide, centre, both, own_charge, other_charge,
         elec_rhs, elec_inv, drop_rhs, drop_inv) = run(
            functools.partial(first_kernel, couple), "coupling_other_half", 4.0,
            (core, *(pltpu.with_memory_space_constraint(value, pltpu.HBM) for value in inputs)),
            [SMEM] + [HBM] * 7,
            outs,
            [pltpu.VMEM(value.shape, value.dtype) for value in inputs[:3]]
            + [pltpu.VMEM((8, drop), f32), pltpu.SemaphoreType.DMA((7,))],
        )
        got = swap(send, core_pairs)
        own_high, own_low, keep, line = run(
            functools.partial(second_kernel, couple), "coupling_own_half", 2.0,
            (wide, centre, both, own_charge, other_charge, other_high, other_low),
            [VMEM] * 7,
            [((elec, half), bf16)] * 2 + [((rows, half), f32), ((rows, elec), f32)],
        )
        parts = sums(line, add(keep, got, line))

        two, both = run(
            functools.partial(middle_kernel, couple), "elec_charges_to_drop_field", 0.8,
            (*parts, elec_rhs, elec_inv, other_high, other_low),
            [VMEM] * 8,
            [((2, rows, half), f32), ((2 * rows, elec), bf16)],
        )
        two_got = swap(two, core_pairs)
        keep, share = run(
            functools.partial(own_kernel, couple), "fields_of_own_half", 1.5,
            (core, both, drop_rhs, drop_inv, two, own_high, own_low),
            [SMEM] + [VMEM] * 6,
            [((rows, half), f32), ((rows, elec), f32)],
        )
        plane, = run(plane_kernel, "add", 0.1, (keep, two_got), [VMEM] * 2, [((rows, half), f32)])
        line, = run(
            functools.partial(other_kernel, couple), "elec_field_of_other_half", 1.0,
            (core, drop_rhs, drop_inv, two_got, share, other_high, other_low),
            [SMEM] + [VMEM] * 6,
            [((rows, elec), f32)],
        )
        parts = sums(line, plane)

        line, plane = run(
            add_pairs_kernel, "add_pairs", 0.1, parts, [VMEM] * 4, [((rows, elec), f32), ((rows, half), f32)]
        )
        plane_got = swap(plane, core_pairs)
        outs = [((rows, elec), f32), ((rows, drop), f32)]
        charge_elec, charge_drop = run(
            charges_kernel, "charges_of_own_half", 1.3,
            (core, elec_rhs, elec_inv, line, drop_rhs, drop_inv, plane),
            [SMEM] + [VMEM] * 6,
            outs,
            [pltpu.VMEM((rows, elec), f32), pltpu.VMEM((rows, half), f32), pltpu.SemaphoreType.DMA((2,))],
            out_spec=HBM,
        )
        charge_drop, = run(
            rest_kernel, "charges_of_other_half", 1.0,
            (core, drop_rhs, drop_inv, plane_got, charge_drop),
            [SMEM] + [VMEM] * 3 + [HBM],
            outs[1:],
            [pltpu.VMEM((rows, half), f32), pltpu.SemaphoreType.DMA((2,))],
            out_spec=HBM,
            aliases={4: 0},
        )
        return (charge_elec, charge_drop)

    placed = (
        P(None, "elec"),
        P(None, "drop"),
        P(None, "drop"),
        P(None, "elec"),
        P(None, "drop"),
        P("elec", None, None),
        P("drop", None, None),
    )
    return jax.shard_map(
        on_device,
        mesh=mesh,
        in_specs=placed,
        out_specs=(P(None, "elec"), P(None, "drop")),
        check_vma=False,
    )
```

```python
import functools
import math

import jax
import jax.numpy as jnp
from jax import lax
from jax.experimental import pallas as pl
from jax.experimental.pallas import tpu as pltpu
from jax.sharding import PartitionSpec as P

SOFTEN = 0.001
SCREEN = 1.0
LANES = 128
CHUNK = 256
PARTS = 2
VMEM = pl.BlockSpec(memory_space=pltpu.VMEM)
SMEM = pl.BlockSpec(memory_space=pltpu.SMEM)
ANY = pl.BlockSpec(memory_space=pl.ANY)
HBM = pl.BlockSpec(memory_space=pltpu.HBM)
ROWS_IN = ((1,), (0,))
ROWS_OUT = ((1,), (1,))


def couple_of(total_drop):
    return 1.0 / (3.0 * math.sqrt(total_drop))


def split(value):
    high = value.astype(jnp.bfloat16)
    low = (value - high.astype(jnp.float32)).astype(jnp.bfloat16)
    return high, low


def stacked(value):
    return jnp.concatenate(split(value), axis=0)


def product(both, weights, contract):
    weight_high, weight_low = weights
    rows = both.shape[0] // 2
    dims = (contract, ((), ()))
    first = lax.dot_general(both, weight_high, dims, preferred_element_type=jnp.float32)
    second = lax.dot_general(both[:rows], weight_low, dims, preferred_element_type=jnp.float32)
    return first[:rows] + (first[rows:] + second)


def solve_block(inverse, values):
    return product(stacked(values), split(inverse), ROWS_OUT)


def solve(inv_ref, values):
    pieces = []
    for at in range(values.shape[1] // LANES):
        pieces.append(solve_block(inv_ref[at], values[:, at * LANES : (at + 1) * LANES]))
    return jnp.concatenate(pieces, axis=1)


def gather(vert_ref, index):
    lane, tile = index % LANES, index // LANES
    found = []
    for axis in range(3):
        total = jnp.zeros(index.shape, jnp.float32)
        for at in range(vert_ref.shape[1] // LANES):
            table = jnp.broadcast_to(vert_ref[axis : axis + 1, at * LANES : (at + 1) * LANES], index.shape)
            total = jnp.where(tile == at, jnp.take_along_axis(table, lane, axis=1), total)
        found.append(total)
    return found


def fill_centres(vert_ref, conn_ref, centre):
    half_block = vert_ref.shape[1]
    for at in range(conn_ref.shape[1] // LANES):
        cols = slice(at * LANES, (at + 1) * LANES)
        corners = gather(vert_ref, conn_ref[:, cols] % half_block)
        for axis in range(3):
            g = corners[axis]
            centre[axis : axis + 1, cols] = (g[0:1] + g[1:2] + g[2:3]) / 3.0


def coupling_chunk(wide, centre, start):
    tiles = []
    for lane in range(start, start + CHUNK, LANES):
        here = slice(lane, lane + LANES)
        dx = wide[0] - centre[0:1, here]
        dy = wide[1] - centre[1:2, here]
        dz = wide[2] - centre[2:3, here]
        square = dx * dx + dy * dy + dz * dz + SOFTEN
        inverse = lax.rsqrt(square)
        tiles.append(jnp.exp((square * inverse) * -SCREEN) * inverse)
    return split(jnp.concatenate(tiles, axis=1))


def columns(place, width):
    return pl.ds(pl.multiple_of(place * width, width), width)


def spread(pos, wide):
    upright = jnp.concatenate([pos, jnp.zeros((LANES - pos.shape[0], pos.shape[1]), jnp.float32)], axis=0).T
    for axis in range(3):
        wide[axis] = jnp.broadcast_to(upright[:, axis : axis + 1], (pos.shape[1], LANES))


def first_kernel(couple, core_ref, pos_hbm, vert_hbm, conn_hbm, erhs_hbm, einv_hbm, drhs_hbm, dinv_hbm,
                 high_ref, low_ref, send_ref, wide_ref, centre_ref, elec_ref, own_ref, other_ref,
                 erhs, einv, drhs, dinv, pos, vert, conn, centre, sems):
    half = high_ref.shape[1]
    blocks = half // LANES
    moves = ((conn_hbm, conn), (vert_hbm, vert), (pos_hbm, pos), (erhs_hbm, erhs), (einv_hbm, einv),
             (drhs_hbm, drhs), (dinv_hbm, dinv))
    copies = [pltpu.make_async_copy(here, there, sems.at[at]) for at, (here, there) in enumerate(moves)]
    for copy in copies:
        copy.start()
    for copy in copies[:3]:
        copy.wait()
    spread(pos[...], wide_ref)
    fill_centres(vert, conn, centre)
    for copy in copies[3:]:
        copy.wait()
    both = stacked(solve(einv, erhs[...]))
    elec_ref[...] = both
    own, other = core_ref[0], 1 - core_ref[0]
    centre_ref[...] = centre[:, columns(own, half)]
    centres = centre[:, columns(other, half)]
    for start in range(0, half, CHUNK):
        cols = slice(start, start + CHUNK)
        weights = coupling_chunk(wide_ref, centres, start)
        high_ref[:, cols], low_ref[:, cols] = weights
        send_ref[:, cols] = product(both, weights, ROWS_IN) * couple
        for place, out_ref in ((own, own_ref), (other, other_ref)):
            block = place * blocks + start // LANES
            here = pl.ds(pl.multiple_of(place * half + start, CHUNK), CHUNK)
            out_ref[:, cols] = stacked(solve(dinv.at[pl.ds(block, CHUNK // LANES)], drhs[:, here]))


def second_kernel(couple, wide_ref, centre_ref, both_ref, own_ref, other_ref, ohigh_ref, olow_ref,
                  high_ref, low_ref, keep_ref, elec_ref):
    total = jnp.zeros(elec_ref.shape, jnp.float32)
    for start in range(0, high_ref.shape[1], CHUNK):
        cols = slice(start, start + CHUNK)
        weights = coupling_chunk(wide_ref, centre_ref, start)
        high_ref[:, cols], low_ref[:, cols] = weights
        keep_ref[:, cols] = product(both_ref[...], weights, ROWS_IN) * couple
        total = total + product(other_ref[:, cols], (ohigh_ref[:, cols], olow_ref[:, cols]), ROWS_OUT)
        total = total + product(own_ref[:, cols], weights, ROWS_OUT)
    elec_ref[...] = total * couple


def drop_charge(place, rhs_ref, inv_ref, field):
    half = field.shape[1]
    blocks = half // LANES
    return solve(inv_ref.at[pl.ds(place * blocks, blocks)], rhs_ref[:, columns(place, half)] - field)


def add_kernel(a_ref, b_ref, *rest):
    rest[-1][...] = a_ref[...] + b_ref[...]


def fill(refs, value):
    rows = refs[0].shape[0]
    for at, ref in enumerate(refs):
        ref[...] = value[at * rows : (at + 1) * rows]


def fold_kernel(a_ref, b_ref, *refs):
    fill(refs[-PARTS:], a_ref[...] + b_ref[...])


def whole(refs):
    return jnp.concatenate([ref[...] for ref in refs], axis=0)


def join_kernel(*refs):
    refs[-1][...] = whole(refs[:PARTS]) + whole(refs[PARTS : 2 * PARTS])


def to_drop_kernel(couple, left_ref, right_ref, rhs_ref, inv_ref, high_ref, low_ref, send_ref, both_ref):
    both = stacked(solve(inv_ref, rhs_ref[...] - (left_ref[...] + right_ref[...])))
    both_ref[...] = both
    send_ref[...] = product(both, (high_ref[...], low_ref[...]), ROWS_IN) * couple


def keep_kernel(couple, both_ref, high_ref, low_ref, keep_ref):
    keep_ref[...] = product(both_ref[...], (high_ref[...], low_ref[...]), ROWS_IN) * couple


def own_kernel(core_ref, rhs_ref, inv_ref, field_ref, high_ref, low_ref, elec_ref):
    charge = drop_charge(core_ref[0], rhs_ref, inv_ref, field_ref[...])
    elec_ref[...] = product(stacked(charge), (high_ref[...], low_ref[...]), ROWS_OUT)


def other_kernel(couple, core_ref, rhs_ref, inv_ref, field_ref, share_ref, high_ref, low_ref, elec_ref):
    charge = drop_charge(1 - core_ref[0], rhs_ref, inv_ref, field_ref[...])
    elec_ref[...] = (share_ref[...] + product(stacked(charge), (high_ref[...], low_ref[...]), ROWS_OUT)) * couple


def charges_kernel(is_other, at, core_ref, rhs_ref, inv_ref, *refs):
    out_ref = refs[-1]
    rows, half = out_ref.shape
    blocks = half // LANES
    place = jnp.abs(core_ref[0] - is_other)
    values = rhs_ref[at * rows : (at + 1) * rows, columns(place, half)] - whole(refs[:-1])
    out_ref[...] = solve(inv_ref.at[pl.ds(place * blocks, blocks)], values)


def last_kernel(core_ref, rhs_ref, inv_ref, own_first_ref, own_last_ref, other_first_ref, left_ref, right_ref, drop_hbm,
                token_ref, other_last, sems):
    token_ref[...] = jnp.zeros_like(token_ref)
    rows, half = other_last.shape
    own, other = columns(core_ref[0], half), columns(1 - core_ref[0], half)
    copies = []
    for at, (ref, part, cols) in enumerate(
        ((own_first_ref, 0, own), (own_last_ref, 1, own), (other_first_ref, 0, other), (other_last, 1, other))
    ):
        if at == 3:
            charges_kernel(1, 1, core_ref, rhs_ref, inv_ref, left_ref, right_ref, other_last)
        place = drop_hbm.at[part * rows : (part + 1) * rows, cols]
        copies.append(pltpu.make_async_copy(ref, place, sems.at[at]))
        copies[-1].start()
    for copy in copies:
        copy.wait()


def elec_kernel(rhs_ref, inv_ref, left_ref, right_ref, after, out_ref):
    out_ref[...] = solve(inv_ref, rhs_ref[...] - (left_ref[...] + right_ref[...]))


def run(kernel, name, micros, operands, specs, outs, scratch=(), out_spec=VMEM, aliases=()):
    return pl.pallas_call(
        kernel,
        out_shape=[jax.ShapeDtypeStruct(shape, dtype) for shape, dtype in outs],
        in_specs=specs,
        out_specs=[out_spec] * len(outs),
        input_output_aliases=dict(aliases),
        scratch_shapes=list(scratch),
        compiler_params=pltpu.CompilerParams(vmem_limit_bytes=32 * 2**20),
        cost_estimate=pl.CostEstimate(flops=0, bytes_accessed=int(micros * 3.3e6), transcendentals=0),
        name=name,
    )(*operands)


def add(left, right, *after):
    return run(
        add_kernel, "add", 0.1, (left, right, *after), [VMEM] * 2 + [ANY] * len(after), [(left.shape, jnp.float32)]
    )[0]


def run_last(core, drop_rhs, drop_inv, done, fields):
    rows, half = done[0].shape
    return pl.pallas_call(
        last_kernel,
        out_shape=[jax.ShapeDtypeStruct(drop_rhs.shape, jnp.float32), jax.ShapeDtypeStruct((8, LANES), jnp.float32)],
        in_specs=[SMEM] + [VMEM] * 7,
        out_specs=[HBM, VMEM],
        scratch_shapes=[pltpu.VMEM((rows, half), jnp.float32), pltpu.SemaphoreType.DMA((4,))],
        compiler_params=pltpu.CompilerParams(vmem_limit_bytes=32 * 2**20),
        name="last_drop_charges",
    )(core, drop_rhs, drop_inv, *done, *fields)


def exchanges(elec_devices, drop_devices):
    def pairs(partner):
        out = []
        for elec in range(elec_devices):
            for drop in range(drop_devices):
                to_elec, to_drop = partner(elec, drop)
                out.append((elec * drop_devices + drop, to_elec * drop_devices + to_drop))
        return out

    def ordered(bits, step, core):
        return bits[step] if core == 0 else bits[len(bits) - 1 - step]

    chip_bits = range(1, elec_devices.bit_length() - 1)
    drop_bits = range(drop_devices.bit_length() - 1)
    core = pairs(lambda e, d: (e ^ 1, d))
    plane = [
        pairs(lambda e, d, s=s: (e ^ (1 << ordered(chip_bits, s, e & 1)), d)) for s in range(len(chip_bits))
    ]
    line = [
        pairs(lambda e, d, s=s: (e, d ^ (1 << ordered(drop_bits, s, e & 1)))) for s in range(len(drop_bits))
    ]
    return core, plane, line


def solution(mesh):
    elec_devices, drop_devices = mesh.shape["elec"], mesh.shape["drop"]
    core_pairs, plane_pairs, line_pairs = exchanges(elec_devices, drop_devices)

    def swap(value, pairs):
        return lax.ppermute(value, ("elec", "drop"), pairs)

    def steps(line, planes):
        for at in range(max(len(line_pairs), len(plane_pairs)) - 1):
            if at < len(line_pairs) - 1:
                line = add(line, swap(line, line_pairs[at]))
            if at < len(plane_pairs) - 1:
                planes = [add(plane, swap(plane, plane_pairs[at])) for plane in planes]
        return (line, swap(line, line_pairs[-1])), [(plane, swap(plane, plane_pairs[-1])) for plane in planes]

    def on_device(elec_pos, drop_vert, drop_conn, elec_rhs, drop_rhs, elec_inv, drop_inv):
        f32, bf16 = jnp.float32, jnp.bfloat16
        rows, elec = elec_rhs.shape
        drop = drop_rhs.shape[1]
        half = drop // 2
        couple = couple_of(drop * drop_devices)
        core = (lax.axis_index("elec") % 2).astype(jnp.int32).reshape(1)

        inputs = (elec_pos, drop_vert, drop_conn, elec_rhs, elec_inv, drop_rhs, drop_inv)
        outs = [((elec, half), bf16)] * 2 + [((rows, half), f32), ((3, elec, LANES), f32), ((8, half), f32)]
        outs += [((2 * rows, elec), bf16)] + [((2 * rows, half), bf16)] * 2 + [(value.shape, f32) for value in inputs[3:]]
        (other_high, other_low, send, wide, centre, both, own_charge, other_charge,
         elec_rhs, elec_inv, drop_rhs, drop_inv) = run(
            functools.partial(first_kernel, couple), "coupling_other_half", 4.0,
            (core, *(pltpu.with_memory_space_constraint(value, pltpu.HBM) for value in inputs)),
            [SMEM] + [HBM] * 7,
            outs,
            [pltpu.VMEM(value.shape, value.dtype) for value in inputs[:3]]
            + [pltpu.VMEM((8, drop), f32), pltpu.SemaphoreType.DMA((7,))],
        )
        got = swap(send, core_pairs)
        own_high, own_low, keep, line = run(
            functools.partial(second_kernel, couple), "coupling_own_half", 2.0,
            (wide, centre, both, own_charge, other_charge, other_high, other_low),
            [VMEM] * 7,
            [((elec, half), bf16)] * 2 + [((rows, half), f32), ((rows, elec), f32)],
        )
        part = rows // PARTS

        def folded(left, right, *after):
            return run(
                fold_kernel, "add", 0.1, (left, right, *after), [VMEM] * 2 + [ANY] * len(after),
                [((part, half), f32)] * PARTS,
            )

        line, planes = steps(line, folded(keep, got, line))

        send, both = run(
            functools.partial(to_drop_kernel, couple), "elec_charges_to_drop_field", 0.8,
            (*line, elec_rhs, elec_inv, other_high, other_low),
            [VMEM] * 6,
            [((rows, half), f32), ((2 * rows, elec), bf16)],
        )
        got = swap(send, core_pairs)
        field, = run(
            join_kernel, "add", 0.1, [pair[at] for at in range(2) for pair in planes], [VMEM] * (2 * PARTS),
            [((rows, half), f32)],
        )
        field_got = swap(field, core_pairs)
        keep, = run(
            functools.partial(keep_kernel, couple), "drop_field_of_own_half", 0.6,
            (both, own_high, own_low), [VMEM] * 3, [((rows, half), f32)],
        )
        share, = run(
            own_kernel, "elec_field_of_own_half", 1.0,
            (core, drop_rhs, drop_inv, field, own_high, own_low),
            [SMEM] + [VMEM] * 5,
            [((rows, elec), f32)],
        )
        line, = run(
            functools.partial(other_kernel, couple), "elec_field_of_other_half", 1.0,
            (core, drop_rhs, drop_inv, field_got, share, other_high, other_low),
            [SMEM] + [VMEM] * 6,
            [((rows, elec), f32)],
        )
        line, planes = steps(line, folded(keep, got))

        def charges(is_other, at, fields):
            return run(
                functools.partial(charges_kernel, is_other, at), "drop_charges", 0.8,
                (core, drop_rhs, drop_inv, *fields), [SMEM] + [VMEM] * (2 + len(fields)), [((part, half), f32)],
            )[0]

        mine, theirs = [], []
        for at, (plane, plane_got) in enumerate(planes):
            after = [charges(0, 0, mine[0])] if at else []
            mine.append(
                run(
                    fold_kernel, "add", 0.1, (plane, plane_got, *after), [VMEM] * 2 + [ANY] * len(after),
                    [((part // 2, half), f32)] * 2,
                )
            )
            theirs.append([swap(value, core_pairs) for value in mine[at]])
            done = after
        done += [charges(0, 1, mine[1]), charges(1, 0, theirs[0])]
        charge_drop, token = run_last(core, drop_rhs, drop_inv, done, theirs[1])
        charge_elec, = run(
            elec_kernel, "elec_charges", 1.0, (elec_rhs, elec_inv, *line, token), [VMEM] * 4 + [ANY],
            [((rows, elec), f32)],
        )
        return (charge_elec, charge_drop)

    placed = (
        P(None, "elec"),
        P(None, "drop"),
        P(None, "drop"),
        P(None, "elec"),
        P(None, "drop"),
        P("elec", None, None),
        P("drop", None, None),
    )
    return jax.shard_map(
        on_device,
        mesh=mesh,
        in_specs=placed,
        out_specs=(P(None, "elec"), P(None, "drop")),
        check_vma=False,
    )
```

```python
import functools
import math

import jax
import jax.numpy as jnp
from jax import lax
from jax.experimental import pallas as pl
from jax.experimental.pallas import tpu as pltpu
from jax.sharding import PartitionSpec as P

SOFTEN = 0.001
SCREEN = 1.0
LANES = 128
CHUNK = 256
PARTS = 2
VMEM = pl.BlockSpec(memory_space=pltpu.VMEM)
SMEM = pl.BlockSpec(memory_space=pltpu.SMEM)
ANY = pl.BlockSpec(memory_space=pl.ANY)
HBM = pl.BlockSpec(memory_space=pltpu.HBM)
ROWS_IN = ((1,), (0,))
ROWS_OUT = ((1,), (1,))


def couple_of(total_drop):
    return 1.0 / (3.0 * math.sqrt(total_drop))


def split(value):
    high = value.astype(jnp.bfloat16)
    low = (value - high.astype(jnp.float32)).astype(jnp.bfloat16)
    return high, low


def stacked(value):
    return jnp.concatenate(split(value), axis=0)


def product(both, weights, contract):
    weight_high, weight_low = weights
    rows = both.shape[0] // 2
    dims = (contract, ((), ()))
    first = lax.dot_general(both, weight_high, dims, preferred_element_type=jnp.float32)
    second = lax.dot_general(both[:rows], weight_low, dims, preferred_element_type=jnp.float32)
    return first[:rows] + (first[rows:] + second)


def solve_block(inverse, values):
    return product(stacked(values), split(inverse), ROWS_OUT)


def solve(inv_ref, values):
    pieces = []
    for at in range(values.shape[1] // LANES):
        pieces.append(solve_block(inv_ref[at], values[:, at * LANES : (at + 1) * LANES]))
    return jnp.concatenate(pieces, axis=1)


def gather(vert_ref, index):
    lane, tile = index % LANES, index // LANES
    found = []
    for axis in range(3):
        total = jnp.zeros(index.shape, jnp.float32)
        for at in range(vert_ref.shape[1] // LANES):
            table = jnp.broadcast_to(vert_ref[axis : axis + 1, at * LANES : (at + 1) * LANES], index.shape)
            total = jnp.where(tile == at, jnp.take_along_axis(table, lane, axis=1), total)
        found.append(total)
    return found


def fill_centres(vert_ref, conn_ref, centre):
    half_block = vert_ref.shape[1]
    for at in range(conn_ref.shape[1] // LANES):
        cols = slice(at * LANES, (at + 1) * LANES)
        corners = gather(vert_ref, conn_ref[:, cols] % half_block)
        for axis in range(3):
            g = corners[axis]
            centre[axis : axis + 1, cols] = (g[0:1] + g[1:2] + g[2:3]) / 3.0


def coupling_chunk(wide, centre, start):
    tiles = []
    for lane in range(start, start + CHUNK, LANES):
        here = slice(lane, lane + LANES)
        dx = wide[0] - centre[0:1, here]
        dy = wide[1] - centre[1:2, here]
        dz = wide[2] - centre[2:3, here]
        square = dx * dx + dy * dy + dz * dz + SOFTEN
        inverse = lax.rsqrt(square)
        tiles.append(jnp.exp((square * inverse) * -SCREEN) * inverse)
    return split(jnp.concatenate(tiles, axis=1))


def columns(place, width):
    return pl.ds(pl.multiple_of(place * width, width), width)


def spread(pos, wide):
    upright = jnp.concatenate([pos, jnp.zeros((LANES - pos.shape[0], pos.shape[1]), jnp.float32)], axis=0).T
    for axis in range(3):
        wide[axis] = jnp.broadcast_to(upright[:, axis : axis + 1], (pos.shape[1], LANES))


def first_kernel(couple, core_ref, pos_hbm, vert_hbm, conn_hbm, erhs_hbm, einv_hbm, drhs_hbm, dinv_hbm,
                 high_ref, low_ref, send_ref, wide_ref, centre_ref, elec_ref, own_ref, other_ref,
                 erhs, einv, drhs, dinv, pos, vert, conn, centre, sems):
    half = high_ref.shape[1]
    blocks = half // LANES
    moves = ((conn_hbm, conn), (vert_hbm, vert), (pos_hbm, pos), (erhs_hbm, erhs), (einv_hbm, einv),
             (drhs_hbm, drhs), (dinv_hbm, dinv))
    copies = [pltpu.make_async_copy(here, there, sems.at[at]) for at, (here, there) in enumerate(moves)]
    for copy in copies:
        copy.start()
    for copy in copies[:3]:
        copy.wait()
    spread(pos[...], wide_ref)
    fill_centres(vert, conn, centre)
    for copy in copies[3:]:
        copy.wait()
    both = stacked(solve(einv, erhs[...]))
    elec_ref[...] = both
    own, other = core_ref[0], 1 - core_ref[0]
    centre_ref[...] = centre[:, columns(own, half)]
    centres = centre[:, columns(other, half)]
    for start in range(0, half, CHUNK):
        cols = slice(start, start + CHUNK)
        weights = coupling_chunk(wide_ref, centres, start)
        high_ref[:, cols], low_ref[:, cols] = weights
        send_ref[:, cols] = product(both, weights, ROWS_IN) * couple
        for place, out_ref in ((own, own_ref), (other, other_ref)):
            block = place * blocks + start // LANES
            here = pl.ds(pl.multiple_of(place * half + start, CHUNK), CHUNK)
            out_ref[:, cols] = stacked(solve(dinv.at[pl.ds(block, CHUNK // LANES)], drhs[:, here]))


def second_kernel(couple, wide_ref, centre_ref, both_ref, own_ref, other_ref, ohigh_ref, olow_ref,
                  high_ref, low_ref, keep_ref, elec_ref):
    total = jnp.zeros(elec_ref.shape, jnp.float32)
    for start in range(0, high_ref.shape[1], CHUNK):
        cols = slice(start, start + CHUNK)
        weights = coupling_chunk(wide_ref, centre_ref, start)
        high_ref[:, cols], low_ref[:, cols] = weights
        keep_ref[:, cols] = product(both_ref[...], weights, ROWS_IN) * couple
        total = total + product(other_ref[:, cols], (ohigh_ref[:, cols], olow_ref[:, cols]), ROWS_OUT)
        total = total + product(own_ref[:, cols], weights, ROWS_OUT)
    elec_ref[...] = total * couple


def drop_charge(place, rhs_ref, inv_ref, field):
    half = field.shape[1]
    blocks = half // LANES
    return solve(inv_ref.at[pl.ds(place * blocks, blocks)], rhs_ref[:, columns(place, half)] - field)


def add_kernel(a_ref, b_ref, *rest):
    rest[-1][...] = a_ref[...] + b_ref[...]


def fill(refs, value):
    rows = refs[0].shape[0]
    for at, ref in enumerate(refs):
        ref[...] = value[at * rows : (at + 1) * rows]


def fold_kernel(a_ref, b_ref, *refs):
    fill(refs[-PARTS:], a_ref[...] + b_ref[...])


def whole(refs):
    return jnp.concatenate([ref[...] for ref in refs], axis=0)


def join_kernel(*refs):
    refs[-1][...] = whole(refs[:PARTS]) + whole(refs[PARTS : 2 * PARTS])


def to_drop_kernel(couple, left_ref, right_ref, rhs_ref, inv_ref, high_ref, low_ref, send_ref, both_ref):
    both = stacked(solve(inv_ref, rhs_ref[...] - (left_ref[...] + right_ref[...])))
    both_ref[...] = both
    send_ref[...] = product(both, (high_ref[...], low_ref[...]), ROWS_IN) * couple


def keep_kernel(couple, both_ref, high_ref, low_ref, keep_ref):
    keep_ref[...] = product(both_ref[...], (high_ref[...], low_ref[...]), ROWS_IN) * couple


def own_kernel(core_ref, rhs_ref, inv_ref, field_ref, high_ref, low_ref, elec_ref):
    charge = drop_charge(core_ref[0], rhs_ref, inv_ref, field_ref[...])
    elec_ref[...] = product(stacked(charge), (high_ref[...], low_ref[...]), ROWS_OUT)


def other_kernel(couple, core_ref, rhs_ref, inv_ref, field_ref, share_ref, high_ref, low_ref, elec_ref):
    charge = drop_charge(1 - core_ref[0], rhs_ref, inv_ref, field_ref[...])
    elec_ref[...] = (share_ref[...] + product(stacked(charge), (high_ref[...], low_ref[...]), ROWS_OUT)) * couple


def charges_kernel(is_other, at, core_ref, rhs_ref, inv_ref, *refs):
    out_ref = refs[-1]
    rows, half = out_ref.shape
    blocks = half // LANES
    place = jnp.abs(core_ref[0] - is_other)
    values = rhs_ref[at * rows : (at + 1) * rows, columns(place, half)] - whole(refs[:-1])
    out_ref[...] = solve(inv_ref.at[pl.ds(place * blocks, blocks)], values)


def last_kernel(core_ref, rhs_ref, inv_ref, own_first_ref, own_last_ref, other_first_ref, left_ref, right_ref, drop_hbm,
                token_ref, other_last, sems):
    token_ref[...] = jnp.zeros_like(token_ref)
    rows, half = other_last.shape
    own, other = columns(core_ref[0], half), columns(1 - core_ref[0], half)
    copies = []
    for at, (ref, part, cols) in enumerate(
        ((own_first_ref, 0, own), (own_last_ref, 1, own), (other_first_ref, 0, other), (other_last, 1, other))
    ):
        if at == 3:
            charges_kernel(1, 1, core_ref, rhs_ref, inv_ref, left_ref, right_ref, other_last)
        place = drop_hbm.at[part * rows : (part + 1) * rows, cols]
        copies.append(pltpu.make_async_copy(ref, place, sems.at[at]))
        copies[-1].start()
    for copy in copies:
        copy.wait()


def elec_kernel(rhs_ref, inv_ref, left_ref, right_ref, after, out_hbm, charge, sems):
    copies = []
    for at in range(inv_ref.shape[0]):
        cols = slice(at * LANES, (at + 1) * LANES)
        charge[:, cols] = solve_block(inv_ref[at], rhs_ref[:, cols] - (left_ref[:, cols] + right_ref[:, cols]))
        copies.append(pltpu.make_async_copy(charge.at[:, cols], out_hbm.at[:, cols], sems.at[at]))
        copies[-1].start()
    for copy in copies:
        copy.wait()


def run(kernel, name, micros, operands, specs, outs, scratch=(), out_spec=VMEM, aliases=()):
    return pl.pallas_call(
        kernel,
        out_shape=[jax.ShapeDtypeStruct(shape, dtype) for shape, dtype in outs],
        in_specs=specs,
        out_specs=[out_spec] * len(outs),
        input_output_aliases=dict(aliases),
        scratch_shapes=list(scratch),
        compiler_params=pltpu.CompilerParams(vmem_limit_bytes=32 * 2**20),
        cost_estimate=pl.CostEstimate(flops=0, bytes_accessed=int(micros * 3.3e6), transcendentals=0),
        name=name,
    )(*operands)


def add(left, right, *after):
    return run(
        add_kernel, "add", 0.1, (left, right, *after), [VMEM] * 2 + [ANY] * len(after), [(left.shape, jnp.float32)]
    )[0]


def run_last(core, drop_rhs, drop_inv, done, fields):
    rows, half = done[0].shape
    return pl.pallas_call(
        last_kernel,
        out_shape=[jax.ShapeDtypeStruct(drop_rhs.shape, jnp.float32), jax.ShapeDtypeStruct((8, LANES), jnp.float32)],
        in_specs=[SMEM] + [VMEM] * 7,
        out_specs=[HBM, VMEM],
        scratch_shapes=[pltpu.VMEM((rows, half), jnp.float32), pltpu.SemaphoreType.DMA((4,))],
        compiler_params=pltpu.CompilerParams(vmem_limit_bytes=32 * 2**20),
        name="last_drop_charges",
    )(core, drop_rhs, drop_inv, *done, *fields)


def exchanges(elec_devices, drop_devices, far_core):
    def pairs(partner):
        out = []
        for elec in range(elec_devices):
            for drop in range(drop_devices):
                to_elec, to_drop = partner(elec, drop)
                out.append((elec * drop_devices + drop, to_elec * drop_devices + to_drop))
        return out

    def ordered(bits, step, core):
        return bits[step] if core == 0 else bits[len(bits) - 1 - step]

    chip_bits = range(1, elec_devices.bit_length() - 1)
    drop_bits = range(drop_devices.bit_length() - 1)
    core = pairs(lambda e, d: (e ^ 1, d))
    plane = [
        pairs(lambda e, d, s=s: (e ^ (1 << ordered(chip_bits, s, e & 1)), d)) for s in range(len(chip_bits))
    ]
    line = [
        pairs(lambda e, d, s=s: (e, d ^ (1 << ordered(drop_bits, s, far_core ^ 1 ^ (e & 1))))) for s in range(len(drop_bits))
    ]
    return core, line, plane


def solution(mesh):
    elec_devices, drop_devices = mesh.shape["elec"], mesh.shape["drop"]
    core_pairs, *first_pairs = exchanges(elec_devices, drop_devices, 0)
    _, *second_pairs = exchanges(elec_devices, drop_devices, 1)

    def swap(value, pairs):
        return lax.ppermute(value, ("elec", "drop"), pairs)

    def steps(line, planes, line_pairs, plane_pairs):
        for at in range(max(len(line_pairs), len(plane_pairs)) - 1):
            if at < len(line_pairs) - 1:
                line = add(line, swap(line, line_pairs[at]))
            if at < len(plane_pairs) - 1:
                planes = [add(plane, swap(plane, plane_pairs[at])) for plane in planes]
        return (line, swap(line, line_pairs[-1])), [(plane, swap(plane, plane_pairs[-1])) for plane in planes]

    def on_device(elec_pos, drop_vert, drop_conn, elec_rhs, drop_rhs, elec_inv, drop_inv):
        f32, bf16 = jnp.float32, jnp.bfloat16
        rows, elec = elec_rhs.shape
        drop = drop_rhs.shape[1]
        half = drop // 2
        couple = couple_of(drop * drop_devices)
        core = (lax.axis_index("elec") % 2).astype(jnp.int32).reshape(1)

        inputs = (elec_pos, drop_vert, drop_conn, elec_rhs, elec_inv, drop_rhs, drop_inv)
        outs = [((elec, half), bf16)] * 2 + [((rows, half), f32), ((3, elec, LANES), f32), ((8, half), f32)]
        outs += [((2 * rows, elec), bf16)] + [((2 * rows, half), bf16)] * 2 + [(value.shape, f32) for value in inputs[3:]]
        (other_high, other_low, send, wide, centre, both, own_charge, other_charge,
         elec_rhs, elec_inv, drop_rhs, drop_inv) = run(
            functools.partial(first_kernel, couple), "coupling_other_half", 4.0,
            (core, *(pltpu.with_memory_space_constraint(value, pltpu.HBM) for value in inputs)),
            [SMEM] + [HBM] * 7,
            outs,
            [pltpu.VMEM(value.shape, value.dtype) for value in inputs[:3]]
            + [pltpu.VMEM((8, drop), f32), pltpu.SemaphoreType.DMA((7,))],
        )
        got = swap(send, core_pairs)
        own_high, own_low, keep, line = run(
            functools.partial(second_kernel, couple), "coupling_own_half", 2.0,
            (wide, centre, both, own_charge, other_charge, other_high, other_low),
            [VMEM] * 7,
            [((elec, half), bf16)] * 2 + [((rows, half), f32), ((rows, elec), f32)],
        )
        part = rows // PARTS

        def folded(left, right, *after):
            return run(
                fold_kernel, "add", 0.1, (left, right, *after), [VMEM] * 2 + [ANY] * len(after),
                [((part, half), f32)] * PARTS,
            )

        line, planes = steps(line, folded(keep, got, line), *first_pairs)

        send, both = run(
            functools.partial(to_drop_kernel, couple), "elec_charges_to_drop_field", 0.8,
            (*line, elec_rhs, elec_inv, other_high, other_low),
            [VMEM] * 6,
            [((rows, half), f32), ((2 * rows, elec), bf16)],
        )
        got = swap(send, core_pairs)
        keep, = run(
            functools.partial(keep_kernel, couple), "drop_field_of_own_half", 0.6,
            (both, own_high, own_low), [VMEM] * 3, [((rows, half), f32)],
        )
        field, = run(
            join_kernel, "add", 0.1, [pair[at] for at in range(2) for pair in planes] + [keep],
            [VMEM] * (2 * PARTS) + [ANY],
            [((rows, half), f32)],
        )
        field_got = swap(field, core_pairs)
        share, = run(
            own_kernel, "elec_field_of_own_half", 1.0,
            (core, drop_rhs, drop_inv, field, own_high, own_low),
            [SMEM] + [VMEM] * 5,
            [((rows, elec), f32)],
        )
        line, = run(
            functools.partial(other_kernel, couple), "elec_field_of_other_half", 1.0,
            (core, drop_rhs, drop_inv, field_got, share, other_high, other_low),
            [SMEM] + [VMEM] * 6,
            [((rows, elec), f32)],
        )
        line, planes = steps(line, folded(keep, got), *second_pairs)

        def charges(is_other, at, fields):
            return run(
                functools.partial(charges_kernel, is_other, at), "drop_charges", 0.8,
                (core, drop_rhs, drop_inv, *fields), [SMEM] + [VMEM] * (2 + len(fields)), [((part, half), f32)],
            )[0]

        mine, theirs = [], []
        for at, (plane, plane_got) in enumerate(planes):
            after = [charges(0, 0, mine[0])] if at else []
            mine.append(
                run(
                    fold_kernel, "add", 0.1, (plane, plane_got, *after), [VMEM] * 2 + [ANY] * len(after),
                    [((part // 2, half), f32)] * 2,
                )
            )
            theirs.append([swap(value, core_pairs) for value in mine[at]])
            done = after
        done += [charges(0, 1, mine[1]), charges(1, 0, theirs[0])]
        charge_drop, token = run_last(core, drop_rhs, drop_inv, done, theirs[1])
        charge_elec, = run(
            elec_kernel, "elec_charges", 1.0, (elec_rhs, elec_inv, *line, token), [VMEM] * 4 + [ANY],
            [((rows, elec), f32)],
            [pltpu.VMEM((rows, elec), f32), pltpu.SemaphoreType.DMA((elec_inv.shape[0],))],
            out_spec=HBM,
        )
        return (charge_elec, charge_drop)

    placed = (
        P(None, "elec"),
        P(None, "drop"),
        P(None, "drop"),
        P(None, "elec"),
        P(None, "drop"),
        P("elec", None, None),
        P("drop", None, None),
    )
    return jax.shard_map(
        on_device,
        mesh=mesh,
        in_specs=placed,
        out_specs=(P(None, "elec"), P(None, "drop")),
        check_vma=False,
    )
```

```python
import functools
import math

import jax
import jax.numpy as jnp
from jax import lax
from jax.experimental import pallas as pl
from jax.experimental.pallas import tpu as pltpu
from jax.sharding import PartitionSpec as P

SOFTEN = 0.001
SCREEN = 1.0
LANES = 128
CHUNK = 256
PARTS = 2
VMEM = pl.BlockSpec(memory_space=pltpu.VMEM)
SMEM = pl.BlockSpec(memory_space=pltpu.SMEM)
ANY = pl.BlockSpec(memory_space=pl.ANY)
HBM = pl.BlockSpec(memory_space=pltpu.HBM)
ROWS_IN = ((1,), (0,))
ROWS_OUT = ((1,), (1,))


def couple_of(total_drop):
    return 1.0 / (3.0 * math.sqrt(total_drop))


def split(value):
    high = value.astype(jnp.bfloat16)
    low = (value - high.astype(jnp.float32)).astype(jnp.bfloat16)
    return high, low


def stacked(value):
    return jnp.concatenate(split(value), axis=0)


def product(both, weights, contract):
    weight_high, weight_low = weights
    rows = both.shape[0] // 2
    dims = (contract, ((), ()))
    first = lax.dot_general(both, weight_high, dims, preferred_element_type=jnp.float32)
    second = lax.dot_general(both[:rows], weight_low, dims, preferred_element_type=jnp.float32)
    return first[:rows] + (first[rows:] + second)


def solve_block(inverse, values):
    return product(stacked(values), split(inverse), ROWS_OUT)


def solve(inv_ref, values):
    pieces = []
    for at in range(values.shape[1] // LANES):
        pieces.append(solve_block(inv_ref[at], values[:, at * LANES : (at + 1) * LANES]))
    return jnp.concatenate(pieces, axis=1)


def gather(vert_ref, index):
    lane, tile = index % LANES, index // LANES
    found = []
    for axis in range(3):
        total = jnp.zeros(index.shape, jnp.float32)
        for at in range(vert_ref.shape[1] // LANES):
            table = jnp.broadcast_to(vert_ref[axis : axis + 1, at * LANES : (at + 1) * LANES], index.shape)
            total = jnp.where(tile == at, jnp.take_along_axis(table, lane, axis=1), total)
        found.append(total)
    return found


def fill_centres(vert_ref, conn_ref, centre):
    half_block = vert_ref.shape[1]
    for at in range(conn_ref.shape[1] // LANES):
        cols = slice(at * LANES, (at + 1) * LANES)
        corners = gather(vert_ref, conn_ref[:, cols] % half_block)
        for axis in range(3):
            g = corners[axis]
            centre[axis : axis + 1, cols] = (g[0:1] + g[1:2] + g[2:3]) / 3.0


def coupling_chunk(wide, centre, start):
    tiles = []
    for lane in range(start, start + CHUNK, LANES):
        here = slice(lane, lane + LANES)
        dx = wide[0] - centre[0:1, here]
        dy = wide[1] - centre[1:2, here]
        dz = wide[2] - centre[2:3, here]
        square = dx * dx + dy * dy + dz * dz + SOFTEN
        inverse = lax.rsqrt(square)
        tiles.append(jnp.exp((square * inverse) * -SCREEN) * inverse)
    return split(jnp.concatenate(tiles, axis=1))


def columns(place, width):
    return pl.ds(pl.multiple_of(place * width, width), width)


def spread(pos, wide):
    upright = jnp.concatenate([pos, jnp.zeros((LANES - pos.shape[0], pos.shape[1]), jnp.float32)], axis=0).T
    for axis in range(3):
        wide[axis] = jnp.broadcast_to(upright[:, axis : axis + 1], (pos.shape[1], LANES))


def first_kernel(couple, core_ref, pos_hbm, vert_hbm, conn_hbm, erhs_hbm, einv_hbm, drhs_hbm, dinv_hbm,
                 high_ref, low_ref, send_ref, wide_ref, centre_ref, elec_ref, own_ref, other_ref,
                 erhs, einv, drhs, dinv, pos, vert, conn, centre, sems):
    half = high_ref.shape[1]
    blocks = half // LANES
    moves = ((conn_hbm, conn), (vert_hbm, vert), (pos_hbm, pos), (erhs_hbm, erhs), (einv_hbm, einv),
             (drhs_hbm, drhs), (dinv_hbm, dinv))
    copies = [pltpu.make_async_copy(here, there, sems.at[at]) for at, (here, there) in enumerate(moves)]
    for copy in copies:
        copy.start()
    for copy in copies[:3]:
        copy.wait()
    spread(pos[...], wide_ref)
    fill_centres(vert, conn, centre)
    for copy in copies[3:]:
        copy.wait()
    both = stacked(solve(einv, erhs[...]))
    elec_ref[...] = both
    own, other = core_ref[0], 1 - core_ref[0]
    centre_ref[...] = centre[:, columns(own, half)]
    centres = centre[:, columns(other, half)]
    for start in range(0, half, CHUNK):
        cols = slice(start, start + CHUNK)
        weights = coupling_chunk(wide_ref, centres, start)
        high_ref[:, cols], low_ref[:, cols] = weights
        send_ref[:, cols] = product(both, weights, ROWS_IN) * couple
        for place, out_ref in ((own, own_ref), (other, other_ref)):
            block = place * blocks + start // LANES
            here = pl.ds(pl.multiple_of(place * half + start, CHUNK), CHUNK)
            out_ref[:, cols] = stacked(solve(dinv.at[pl.ds(block, CHUNK // LANES)], drhs[:, here]))


def second_kernel(couple, wide_ref, centre_ref, both_ref, own_ref, other_ref, ohigh_ref, olow_ref,
                  high_ref, low_ref, keep_ref, elec_ref):
    total = jnp.zeros(elec_ref.shape, jnp.float32)
    for start in range(0, high_ref.shape[1], CHUNK):
        cols = slice(start, start + CHUNK)
        weights = coupling_chunk(wide_ref, centre_ref, start)
        high_ref[:, cols], low_ref[:, cols] = weights
        keep_ref[:, cols] = product(both_ref[...], weights, ROWS_IN) * couple
        total = total + product(other_ref[:, cols], (ohigh_ref[:, cols], olow_ref[:, cols]), ROWS_OUT)
        total = total + product(own_ref[:, cols], weights, ROWS_OUT)
    elec_ref[...] = total * couple


def drop_charge(place, rhs_ref, inv_ref, field):
    half = field.shape[1]
    blocks = half // LANES
    return solve(inv_ref.at[pl.ds(place * blocks, blocks)], rhs_ref[:, columns(place, half)] - field)


def add_kernel(a_ref, b_ref, *rest):
    rest[-1][...] = a_ref[...] + b_ref[...]


def fill(refs, value):
    rows = refs[0].shape[0]
    for at, ref in enumerate(refs):
        ref[...] = value[at * rows : (at + 1) * rows]


def fold_kernel(a_ref, b_ref, *refs):
    fill(refs[-PARTS:], a_ref[...] + b_ref[...])


def whole(refs):
    return jnp.concatenate([ref[...] for ref in refs], axis=0)


def drop_kernel(core_ref, rhs_ref, inv_ref, *refs):
    field = whole(refs[:PARTS]) + whole(refs[PARTS : 2 * PARTS])
    refs[-1][...] = drop_charge(core_ref[0], rhs_ref, inv_ref, field)


def to_drop_kernel(couple, left_ref, right_ref, rhs_ref, inv_ref, high_ref, low_ref, send_ref, both_ref):
    both = stacked(solve(inv_ref, rhs_ref[...] - (left_ref[...] + right_ref[...])))
    both_ref[...] = both
    send_ref[...] = product(both, (high_ref[...], low_ref[...]), ROWS_IN) * couple


def keep_kernel(couple, both_ref, high_ref, low_ref, keep_ref):
    keep_ref[...] = product(both_ref[...], (high_ref[...], low_ref[...]), ROWS_IN) * couple


def own_kernel(charge_ref, high_ref, low_ref, elec_ref):
    elec_ref[...] = product(stacked(charge_ref[...]), (high_ref[...], low_ref[...]), ROWS_OUT)


def other_kernel(couple, charge_ref, share_ref, high_ref, low_ref, elec_ref):
    field = product(stacked(charge_ref[...]), (high_ref[...], low_ref[...]), ROWS_OUT)
    elec_ref[...] = (share_ref[...] + field) * couple


def charges_kernel(is_other, at, core_ref, rhs_ref, inv_ref, *refs):
    out_ref = refs[-1]
    rows, half = out_ref.shape
    blocks = half // LANES
    place = jnp.abs(core_ref[0] - is_other)
    values = rhs_ref[at * rows : (at + 1) * rows, columns(place, half)] - whole(refs[:-1])
    out_ref[...] = solve(inv_ref.at[pl.ds(place * blocks, blocks)], values)


def last_kernel(core_ref, rhs_ref, inv_ref, own_first_ref, own_last_ref, other_first_ref, left_ref, right_ref, drop_hbm,
                token_ref, other_last, sems):
    token_ref[...] = jnp.zeros_like(token_ref)
    rows, half = other_last.shape
    own, other = columns(core_ref[0], half), columns(1 - core_ref[0], half)
    copies = []
    for at, (ref, part, cols) in enumerate(
        ((own_first_ref, 0, own), (own_last_ref, 1, own), (other_first_ref, 0, other), (other_last, 1, other))
    ):
        if at == 3:
            charges_kernel(1, 1, core_ref, rhs_ref, inv_ref, left_ref, right_ref, other_last)
        place = drop_hbm.at[part * rows : (part + 1) * rows, cols]
        copies.append(pltpu.make_async_copy(ref, place, sems.at[at]))
        copies[-1].start()
    for copy in copies:
        copy.wait()


def elec_kernel(rhs_ref, inv_ref, left_ref, right_ref, after, out_hbm, charge, sems):
    copies = []
    for at in range(inv_ref.shape[0]):
        cols = slice(at * LANES, (at + 1) * LANES)
        charge[:, cols] = solve_block(inv_ref[at], rhs_ref[:, cols] - (left_ref[:, cols] + right_ref[:, cols]))
        copies.append(pltpu.make_async_copy(charge.at[:, cols], out_hbm.at[:, cols], sems.at[at]))
        copies[-1].start()
    for copy in copies:
        copy.wait()


def run(kernel, name, micros, operands, specs, outs, scratch=(), out_spec=VMEM, aliases=()):
    return pl.pallas_call(
        kernel,
        out_shape=[jax.ShapeDtypeStruct(shape, dtype) for shape, dtype in outs],
        in_specs=specs,
        out_specs=[out_spec] * len(outs),
        input_output_aliases=dict(aliases),
        scratch_shapes=list(scratch),
        compiler_params=pltpu.CompilerParams(vmem_limit_bytes=32 * 2**20),
        cost_estimate=pl.CostEstimate(flops=0, bytes_accessed=int(micros * 3.3e6), transcendentals=0),
        name=name,
    )(*operands)


def add(left, right, *after):
    return run(
        add_kernel, "add", 0.1, (left, right, *after), [VMEM] * 2 + [ANY] * len(after), [(left.shape, jnp.float32)]
    )[0]


def run_last(core, drop_rhs, drop_inv, done, fields):
    rows, half = done[0].shape
    return pl.pallas_call(
        last_kernel,
        out_shape=[jax.ShapeDtypeStruct(drop_rhs.shape, jnp.float32), jax.ShapeDtypeStruct((8, LANES), jnp.float32)],
        in_specs=[SMEM] + [VMEM] * 7,
        out_specs=[HBM, VMEM],
        scratch_shapes=[pltpu.VMEM((rows, half), jnp.float32), pltpu.SemaphoreType.DMA((4,))],
        compiler_params=pltpu.CompilerParams(vmem_limit_bytes=32 * 2**20),
        name="last_drop_charges",
    )(core, drop_rhs, drop_inv, *done, *fields)


def exchanges(elec_devices, drop_devices, far_core):
    def pairs(partner):
        out = []
        for elec in range(elec_devices):
            for drop in range(drop_devices):
                to_elec, to_drop = partner(elec, drop)
                out.append((elec * drop_devices + drop, to_elec * drop_devices + to_drop))
        return out

    def ordered(bits, step, core):
        return bits[step] if core == 0 else bits[len(bits) - 1 - step]

    chip_bits = range(1, elec_devices.bit_length() - 1)
    drop_bits = range(drop_devices.bit_length() - 1)
    core = pairs(lambda e, d: (e ^ 1, d))
    plane = [
        pairs(lambda e, d, s=s: (e ^ (1 << ordered(chip_bits, s, e & 1)), d)) for s in range(len(chip_bits))
    ]
    line = [
        pairs(lambda e, d, s=s: (e, d ^ (1 << ordered(drop_bits, s, far_core ^ 1 ^ (e & 1))))) for s in range(len(drop_bits))
    ]
    return core, line, plane


def solution(mesh):
    elec_devices, drop_devices = mesh.shape["elec"], mesh.shape["drop"]
    core_pairs, *first_pairs = exchanges(elec_devices, drop_devices, 1)
    _, *second_pairs = exchanges(elec_devices, drop_devices, 0)

    def swap(value, pairs):
        return lax.ppermute(value, ("elec", "drop"), pairs)

    def steps(line, planes, line_pairs, plane_pairs):
        for at in range(max(len(line_pairs), len(plane_pairs)) - 1):
            if at < len(line_pairs) - 1:
                line = add(line, swap(line, line_pairs[at]))
            if at < len(plane_pairs) - 1:
                planes = [add(plane, swap(plane, plane_pairs[at])) for plane in planes]
        return (line, swap(line, line_pairs[-1])), [(plane, swap(plane, plane_pairs[-1])) for plane in planes]

    def on_device(elec_pos, drop_vert, drop_conn, elec_rhs, drop_rhs, elec_inv, drop_inv):
        f32, bf16 = jnp.float32, jnp.bfloat16
        rows, elec = elec_rhs.shape
        drop = drop_rhs.shape[1]
        half = drop // 2
        couple = couple_of(drop * drop_devices)
        core = (lax.axis_index("elec") % 2).astype(jnp.int32).reshape(1)

        inputs = (elec_pos, drop_vert, drop_conn, elec_rhs, elec_inv, drop_rhs, drop_inv)
        outs = [((elec, half), bf16)] * 2 + [((rows, half), f32), ((3, elec, LANES), f32), ((8, half), f32)]
        outs += [((2 * rows, elec), bf16)] + [((2 * rows, half), bf16)] * 2 + [(value.shape, f32) for value in inputs[3:]]
        (other_high, other_low, send, wide, centre, both, own_charge, other_charge,
         elec_rhs, elec_inv, drop_rhs, drop_inv) = run(
            functools.partial(first_kernel, couple), "coupling_other_half", 4.0,
            (core, *(pltpu.with_memory_space_constraint(value, pltpu.HBM) for value in inputs)),
            [SMEM] + [HBM] * 7,
            outs,
            [pltpu.VMEM(value.shape, value.dtype) for value in inputs[:3]]
            + [pltpu.VMEM((8, drop), f32), pltpu.SemaphoreType.DMA((7,))],
        )
        got = swap(send, core_pairs)
        own_high, own_low, keep, line = run(
            functools.partial(second_kernel, couple), "coupling_own_half", 2.0,
            (wide, centre, both, own_charge, other_charge, other_high, other_low),
            [VMEM] * 7,
            [((elec, half), bf16)] * 2 + [((rows, half), f32), ((rows, elec), f32)],
        )
        part = rows // PARTS

        def folded(left, right, *after):
            return run(
                fold_kernel, "add", 0.1, (left, right, *after), [VMEM] * 2 + [ANY] * len(after),
                [((part, half), f32)] * PARTS,
            )

        line, planes = steps(line, folded(keep, got, line), *first_pairs)

        send, both = run(
            functools.partial(to_drop_kernel, couple), "elec_charges_to_drop_field", 0.8,
            (*line, elec_rhs, elec_inv, other_high, other_low),
            [VMEM] * 6,
            [((rows, half), f32), ((2 * rows, elec), bf16)],
        )
        got = swap(send, core_pairs)
        keep, = run(
            functools.partial(keep_kernel, couple), "drop_field_of_own_half", 0.6,
            (both, own_high, own_low), [VMEM] * 3, [((rows, half), f32)],
        )
        charge, = run(
            drop_kernel, "drop_charges_of_own_half", 0.4,
            (core, drop_rhs, drop_inv, *(pair[at] for at in range(2) for pair in planes), keep),
            [SMEM] + [VMEM] * (2 + 2 * PARTS) + [ANY],
            [((rows, half), f32)],
        )
        charge_got = swap(charge, core_pairs)
        share, = run(
            own_kernel, "elec_field_of_own_half", 0.8, (charge, own_high, own_low), [VMEM] * 3, [((rows, elec), f32)]
        )
        line, = run(
            functools.partial(other_kernel, couple), "elec_field_of_other_half", 0.8,
            (charge_got, share, other_high, other_low),
            [VMEM] * 4,
            [((rows, elec), f32)],
        )
        line, planes = steps(line, folded(keep, got), *second_pairs)

        def charges(is_other, at, fields):
            return run(
                functools.partial(charges_kernel, is_other, at), "drop_charges", 0.8,
                (core, drop_rhs, drop_inv, *fields), [SMEM] + [VMEM] * (2 + len(fields)), [((part, half), f32)],
            )[0]

        mine, theirs = [], []
        for at, (plane, plane_got) in enumerate(planes):
            after = [charges(0, 0, mine[0])] if at else []
            mine.append(
                run(
                    fold_kernel, "add", 0.1, (plane, plane_got, *after), [VMEM] * 2 + [ANY] * len(after),
                    [((part // 2, half), f32)] * 2,
                )
            )
            theirs.append([swap(value, core_pairs) for value in mine[at]])
            done = after
        done += [charges(0, 1, mine[1]), charges(1, 0, theirs[0])]
        charge_drop, token = run_last(core, drop_rhs, drop_inv, done, theirs[1])
        charge_elec, = run(
            elec_kernel, "elec_charges", 1.0, (elec_rhs, elec_inv, *line, token), [VMEM] * 4 + [ANY],
            [((rows, elec), f32)],
            [pltpu.VMEM((rows, elec), f32), pltpu.SemaphoreType.DMA((elec_inv.shape[0],))],
            out_spec=HBM,
        )
        return (charge_elec, charge_drop)

    placed = (
        P(None, "elec"),
        P(None, "drop"),
        P(None, "drop"),
        P(None, "elec"),
        P(None, "drop"),
        P("elec", None, None),
        P("drop", None, None),
    )
    return jax.shard_map(
        on_device,
        mesh=mesh,
        in_specs=placed,
        out_specs=(P(None, "elec"), P(None, "drop")),
        check_vma=False,
    )
```

```python
import functools
import math

import jax
import jax.numpy as jnp
from jax import lax
from jax.experimental import pallas as pl
from jax.experimental.pallas import tpu as pltpu
from jax.sharding import PartitionSpec as P

SOFTEN = 0.001
SCREEN = 1.0
LANES = 128
CHUNK = 256
PARTS = 2
VMEM = pl.BlockSpec(memory_space=pltpu.VMEM)
SMEM = pl.BlockSpec(memory_space=pltpu.SMEM)
ANY = pl.BlockSpec(memory_space=pl.ANY)
HBM = pl.BlockSpec(memory_space=pltpu.HBM)
ROWS_IN = ((1,), (0,))
ROWS_OUT = ((1,), (1,))


def couple_of(total_drop):
    return 1.0 / (3.0 * math.sqrt(total_drop))


def split(value):
    high = value.astype(jnp.bfloat16)
    low = (value - high.astype(jnp.float32)).astype(jnp.bfloat16)
    return high, low


def stacked(value):
    return jnp.concatenate(split(value), axis=0)


def product(both, weights, contract):
    weight_high, weight_low = weights
    rows = both.shape[0] // 2
    dims = (contract, ((), ()))
    first = lax.dot_general(both, weight_high, dims, preferred_element_type=jnp.float32)
    second = lax.dot_general(both[:rows], weight_low, dims, preferred_element_type=jnp.float32)
    return first[:rows] + (first[rows:] + second)


def solve_block(inverse, values):
    return product(stacked(values), split(inverse), ROWS_OUT)


def solve(inv_ref, values):
    pieces = []
    for at in range(values.shape[1] // LANES):
        pieces.append(solve_block(inv_ref[at], values[:, at * LANES : (at + 1) * LANES]))
    return jnp.concatenate(pieces, axis=1)


def gather(vert_ref, index):
    lane, tile = index % LANES, index // LANES
    found = []
    for axis in range(3):
        total = jnp.zeros(index.shape, jnp.float32)
        for at in range(vert_ref.shape[1] // LANES):
            table = jnp.broadcast_to(vert_ref[axis : axis + 1, at * LANES : (at + 1) * LANES], index.shape)
            total = jnp.where(tile == at, jnp.take_along_axis(table, lane, axis=1), total)
        found.append(total)
    return found


def fill_centres(vert_ref, conn_ref, centre):
    half_block = vert_ref.shape[1]
    for at in range(conn_ref.shape[1] // LANES):
        cols = slice(at * LANES, (at + 1) * LANES)
        corners = gather(vert_ref, conn_ref[:, cols] % half_block)
        for axis in range(3):
            g = corners[axis]
            centre[axis : axis + 1, cols] = (g[0:1] + g[1:2] + g[2:3]) / 3.0


def coupling_chunk(wide, centre, start):
    tiles = []
    for lane in range(start, start + CHUNK, LANES):
        here = slice(lane, lane + LANES)
        dx = wide[0] - centre[0:1, here]
        dy = wide[1] - centre[1:2, here]
        dz = wide[2] - centre[2:3, here]
        square = dx * dx + dy * dy + dz * dz + SOFTEN
        inverse = lax.rsqrt(square)
        tiles.append(jnp.exp((square * inverse) * -SCREEN) * inverse)
    return split(jnp.concatenate(tiles, axis=1))


def columns(place, width):
    return pl.ds(pl.multiple_of(place * width, width), width)


def spread(pos, wide):
    upright = jnp.concatenate([pos, jnp.zeros((LANES - pos.shape[0], pos.shape[1]), jnp.float32)], axis=0).T
    for axis in range(3):
        wide[axis] = jnp.broadcast_to(upright[:, axis : axis + 1], (pos.shape[1], LANES))


def first_kernel(couple, core_ref, pos_hbm, vert_hbm, conn_hbm, erhs_hbm, einv_hbm, drhs_hbm, dinv_hbm,
                 high_ref, low_ref, send_ref, wide_ref, centre_ref, elec_ref, own_ref, other_ref,
                 erhs, einv, drhs, dinv, pos, vert, conn, centre, sems):
    half = high_ref.shape[1]
    blocks = half // LANES
    moves = ((conn_hbm, conn), (vert_hbm, vert), (pos_hbm, pos), (erhs_hbm, erhs), (einv_hbm, einv),
             (drhs_hbm, drhs), (dinv_hbm, dinv))
    copies = [pltpu.make_async_copy(here, there, sems.at[at]) for at, (here, there) in enumerate(moves)]
    for copy in copies:
        copy.start()
    for copy in copies[:3]:
        copy.wait()
    spread(pos[...], wide_ref)
    fill_centres(vert, conn, centre)
    for copy in copies[3:]:
        copy.wait()
    both = stacked(solve(einv, erhs[...]))
    elec_ref[...] = both
    own, other = core_ref[0], 1 - core_ref[0]
    centre_ref[...] = centre[:, columns(own, half)]
    centres = centre[:, columns(other, half)]
    for start in range(0, half, CHUNK):
        cols = slice(start, start + CHUNK)
        weights = coupling_chunk(wide_ref, centres, start)
        high_ref[:, cols], low_ref[:, cols] = weights
        send_ref[:, cols] = product(both, weights, ROWS_IN) * couple
        for place, out_ref in ((own, own_ref), (other, other_ref)):
            block = place * blocks + start // LANES
            here = pl.ds(pl.multiple_of(place * half + start, CHUNK), CHUNK)
            out_ref[:, cols] = stacked(solve(dinv.at[pl.ds(block, CHUNK // LANES)], drhs[:, here]))


def second_kernel(couple, wide_ref, centre_ref, own_ref, other_ref, ohigh_ref, olow_ref,
                  high_ref, low_ref, elec_ref):
    total = jnp.zeros(elec_ref.shape, jnp.float32)
    for start in range(0, high_ref.shape[1], CHUNK):
        cols = slice(start, start + CHUNK)
        weights = coupling_chunk(wide_ref, centre_ref, start)
        high_ref[:, cols], low_ref[:, cols] = weights
        total = total + product(other_ref[:, cols], (ohigh_ref[:, cols], olow_ref[:, cols]), ROWS_OUT)
        total = total + product(own_ref[:, cols], weights, ROWS_OUT)
    elec_ref[...] = total * couple


def drop_charge(place, rhs_ref, inv_ref, field):
    half = field.shape[1]
    blocks = half // LANES
    return solve(inv_ref.at[pl.ds(place * blocks, blocks)], rhs_ref[:, columns(place, half)] - field)


def add_kernel(a_ref, b_ref, *rest):
    rest[-1][...] = a_ref[...] + b_ref[...]


def fill(refs, value):
    rows = refs[0].shape[0]
    for at, ref in enumerate(refs):
        ref[...] = value[at * rows : (at + 1) * rows]


def fold_kernel(a_ref, b_ref, *refs):
    fill(refs[-PARTS:], a_ref[...] + b_ref[...])


def whole(refs):
    return jnp.concatenate([ref[...] for ref in refs], axis=0)


def drop_kernel(core_ref, rhs_ref, inv_ref, *refs):
    field = whole(refs[:PARTS]) + whole(refs[PARTS : 2 * PARTS])
    refs[-1][...] = drop_charge(core_ref[0], rhs_ref, inv_ref, field)


def to_drop_kernel(couple, left_ref, right_ref, rhs_ref, inv_ref, high_ref, low_ref, send_ref, both_ref):
    both = stacked(solve(inv_ref, rhs_ref[...] - (left_ref[...] + right_ref[...])))
    both_ref[...] = both
    send_ref[...] = product(both, (high_ref[...], low_ref[...]), ROWS_IN) * couple


def keep_kernel(couple, both_ref, high_ref, low_ref, keep_ref):
    keep_ref[...] = product(both_ref[...], (high_ref[...], low_ref[...]), ROWS_IN) * couple


def own_kernel(charge_ref, high_ref, low_ref, elec_ref):
    elec_ref[...] = product(stacked(charge_ref[...]), (high_ref[...], low_ref[...]), ROWS_OUT)


def other_kernel(couple, charge_ref, share_ref, high_ref, low_ref, elec_ref):
    field = product(stacked(charge_ref[...]), (high_ref[...], low_ref[...]), ROWS_OUT)
    elec_ref[...] = (share_ref[...] + field) * couple


def charges_kernel(is_other, at, core_ref, rhs_ref, inv_ref, *refs):
    out_ref = refs[-1]
    rows, half = out_ref.shape
    blocks = half // LANES
    place = jnp.abs(core_ref[0] - is_other)
    values = rhs_ref[at * rows : (at + 1) * rows, columns(place, half)] - whole(refs[:-1])
    out_ref[...] = solve(inv_ref.at[pl.ds(place * blocks, blocks)], values)


def last_kernel(core_ref, rhs_ref, inv_ref, own_first_ref, own_last_ref, other_first_ref, left_ref, right_ref, drop_hbm,
                token_ref, other_last, sems):
    token_ref[...] = jnp.zeros_like(token_ref)
    rows, half = other_last.shape
    own, other = columns(core_ref[0], half), columns(1 - core_ref[0], half)
    copies = []
    for at, (ref, part, cols) in enumerate(
        ((own_first_ref, 0, own), (own_last_ref, 1, own), (other_first_ref, 0, other), (other_last, 1, other))
    ):
        if at == 3:
            charges_kernel(1, 1, core_ref, rhs_ref, inv_ref, left_ref, right_ref, other_last)
        place = drop_hbm.at[part * rows : (part + 1) * rows, cols]
        copies.append(pltpu.make_async_copy(ref, place, sems.at[at]))
        copies[-1].start()
    for copy in copies:
        copy.wait()


def elec_kernel(rhs_ref, inv_ref, left_ref, right_ref, after, out_hbm, charge, sems):
    both = stacked(rhs_ref[...] - (left_ref[...] + right_ref[...]))
    copies = []
    blocks = inv_ref.shape[0]
    for at in range(blocks):
        cols = slice(at * LANES, (at + 1) * LANES)
        charge[:, cols] = product(both[:, cols], split(inv_ref[at]), ROWS_OUT)
        if at % 2:
            two = slice((at - 1) * LANES, (at + 1) * LANES)
            copies.append(pltpu.make_async_copy(charge.at[:, two], out_hbm.at[:, two], sems.at[at]))
            copies[-1].start()
    for copy in copies:
        copy.wait()


def run(kernel, name, micros, operands, specs, outs, scratch=(), out_spec=VMEM, aliases=()):
    return pl.pallas_call(
        kernel,
        out_shape=[jax.ShapeDtypeStruct(shape, dtype) for shape, dtype in outs],
        in_specs=specs,
        out_specs=[out_spec] * len(outs),
        input_output_aliases=dict(aliases),
        scratch_shapes=list(scratch),
        compiler_params=pltpu.CompilerParams(vmem_limit_bytes=32 * 2**20),
        cost_estimate=pl.CostEstimate(flops=0, bytes_accessed=int(micros * 3.3e6), transcendentals=0),
        name=name,
    )(*operands)


def add(left, right, *after):
    return run(
        add_kernel, "add", 0.1, (left, right, *after), [VMEM] * 2 + [ANY] * len(after), [(left.shape, jnp.float32)]
    )[0]


def run_last(core, drop_rhs, drop_inv, done, fields):
    rows, half = done[0].shape
    return pl.pallas_call(
        last_kernel,
        out_shape=[jax.ShapeDtypeStruct(drop_rhs.shape, jnp.float32), jax.ShapeDtypeStruct((8, LANES), jnp.float32)],
        in_specs=[SMEM] + [VMEM] * 7,
        out_specs=[HBM, VMEM],
        scratch_shapes=[pltpu.VMEM((rows, half), jnp.float32), pltpu.SemaphoreType.DMA((4,))],
        compiler_params=pltpu.CompilerParams(vmem_limit_bytes=32 * 2**20),
        name="last_drop_charges",
    )(core, drop_rhs, drop_inv, *done, *fields)


def exchanges(elec_devices, drop_devices, far_core):
    def pairs(partner):
        out = []
        for elec in range(elec_devices):
            for drop in range(drop_devices):
                to_elec, to_drop = partner(elec, drop)
                out.append((elec * drop_devices + drop, to_elec * drop_devices + to_drop))
        return out

    def ordered(bits, step, core):
        return bits[step] if core == 0 else bits[len(bits) - 1 - step]

    chip_bits = range(1, elec_devices.bit_length() - 1)
    drop_bits = range(drop_devices.bit_length() - 1)
    core = pairs(lambda e, d: (e ^ 1, d))
    plane = [
        pairs(lambda e, d, s=s: (e ^ (1 << ordered(chip_bits, s, e & 1)), d)) for s in range(len(chip_bits))
    ]
    line = [
        pairs(lambda e, d, s=s: (e, d ^ (1 << ordered(drop_bits, s, far_core ^ 1 ^ (e & 1))))) for s in range(len(drop_bits))
    ]
    return core, line, plane


def solution(mesh):
    elec_devices, drop_devices = mesh.shape["elec"], mesh.shape["drop"]
    core_pairs, *first_pairs = exchanges(elec_devices, drop_devices, 1)
    _, *second_pairs = exchanges(elec_devices, drop_devices, 0)

    def swap(value, pairs):
        return lax.ppermute(value, ("elec", "drop"), pairs)

    def steps(line, planes, line_pairs, plane_pairs):
        for at in range(max(len(line_pairs), len(plane_pairs)) - 1):
            if at < len(line_pairs) - 1:
                line = add(line, swap(line, line_pairs[at]))
            if at < len(plane_pairs) - 1:
                planes = [add(plane, swap(plane, plane_pairs[at])) for plane in planes]
        return (line, swap(line, line_pairs[-1])), [(plane, swap(plane, plane_pairs[-1])) for plane in planes]

    def on_device(elec_pos, drop_vert, drop_conn, elec_rhs, drop_rhs, elec_inv, drop_inv):
        f32, bf16 = jnp.float32, jnp.bfloat16
        rows, elec = elec_rhs.shape
        drop = drop_rhs.shape[1]
        half = drop // 2
        couple = couple_of(drop * drop_devices)
        core = (lax.axis_index("elec") % 2).astype(jnp.int32).reshape(1)

        inputs = (elec_pos, drop_vert, drop_conn, elec_rhs, elec_inv, drop_rhs, drop_inv)
        outs = [((elec, half), bf16)] * 2 + [((rows, half), f32), ((3, elec, LANES), f32), ((8, half), f32)]
        outs += [((2 * rows, elec), bf16)] + [((2 * rows, half), bf16)] * 2 + [(value.shape, f32) for value in inputs[3:]]
        (other_high, other_low, send, wide, centre, both, own_charge, other_charge,
         elec_rhs, elec_inv, drop_rhs, drop_inv) = run(
            functools.partial(first_kernel, couple), "coupling_other_half", 4.0,
            (core, *(pltpu.with_memory_space_constraint(value, pltpu.HBM) for value in inputs)),
            [SMEM] + [HBM] * 7,
            outs,
            [pltpu.VMEM(value.shape, value.dtype) for value in inputs[:3]]
            + [pltpu.VMEM((8, drop), f32), pltpu.SemaphoreType.DMA((7,))],
        )
        got = swap(send, core_pairs)
        own_high, own_low, line = run(
            functools.partial(second_kernel, couple), "coupling_own_half", 2.0,
            (wide, centre, own_charge, other_charge, other_high, other_low),
            [VMEM] * 6,
            [((elec, half), bf16)] * 2 + [((rows, elec), f32)],
        )
        keep, = run(
            functools.partial(keep_kernel, couple), "drop_field_of_own_half", 0.6,
            (both, own_high, own_low), [VMEM] * 3, [((rows, half), f32)],
        )
        part = rows // PARTS

        def folded(left, right, *after):
            return run(
                fold_kernel, "add", 0.1, (left, right, *after), [VMEM] * 2 + [ANY] * len(after),
                [((part, half), f32)] * PARTS,
            )

        line, planes = steps(line, folded(keep, got, line), *first_pairs)

        send, both = run(
            functools.partial(to_drop_kernel, couple), "elec_charges_to_drop_field", 0.8,
            (*line, elec_rhs, elec_inv, other_high, other_low),
            [VMEM] * 6,
            [((rows, half), f32), ((2 * rows, elec), bf16)],
        )
        got = swap(send, core_pairs)
        keep, = run(
            functools.partial(keep_kernel, couple), "drop_field_of_own_half", 0.6,
            (both, own_high, own_low), [VMEM] * 3, [((rows, half), f32)],
        )
        charge, = run(
            drop_kernel, "drop_charges_of_own_half", 0.4,
            (core, drop_rhs, drop_inv, *(pair[at] for at in range(2) for pair in planes), keep),
            [SMEM] + [VMEM] * (2 + 2 * PARTS) + [ANY],
            [((rows, half), f32)],
        )
        charge_got = swap(charge, core_pairs)
        share, = run(
            own_kernel, "elec_field_of_own_half", 0.8, (charge, own_high, own_low), [VMEM] * 3, [((rows, elec), f32)]
        )
        line, = run(
            functools.partial(other_kernel, couple), "elec_field_of_other_half", 0.8,
            (charge_got, share, other_high, other_low),
            [VMEM] * 4,
            [((rows, elec), f32)],
        )
        line, planes = steps(line, folded(keep, got), *second_pairs)

        def charges(is_other, at, fields):
            return run(
                functools.partial(charges_kernel, is_other, at), "drop_charges", 0.8,
                (core, drop_rhs, drop_inv, *fields), [SMEM] + [VMEM] * (2 + len(fields)), [((part, half), f32)],
            )[0]

        mine, theirs = [], []
        for at, (plane, plane_got) in enumerate(planes):
            after = [charges(0, 0, mine[0])] if at else []
            mine.append(
                run(
                    fold_kernel, "add", 0.1, (plane, plane_got, *after), [VMEM] * 2 + [ANY] * len(after),
                    [((part // 2, half), f32)] * 2,
                )
            )
            theirs.append([swap(value, core_pairs) for value in mine[at]])
            done = after
        done += [charges(0, 1, mine[1]), charges(1, 0, theirs[0])]
        charge_drop, token = run_last(core, drop_rhs, drop_inv, done, theirs[1])
        charge_elec, = run(
            elec_kernel, "elec_charges", 1.0, (elec_rhs, elec_inv, *line, token), [VMEM] * 4 + [ANY],
            [((rows, elec), f32)],
            [pltpu.VMEM((rows, elec), f32), pltpu.SemaphoreType.DMA((elec_inv.shape[0],))],
            out_spec=HBM,
        )
        return (charge_elec, charge_drop)

    placed = (
        P(None, "elec"),
        P(None, "drop"),
        P(None, "drop"),
        P(None, "elec"),
        P(None, "drop"),
        P("elec", None, None),
        P("drop", None, None),
    )
    return jax.shard_map(
        on_device,
        mesh=mesh,
        in_specs=placed,
        out_specs=(P(None, "elec"), P(None, "drop")),
        check_vma=False,
    )
```
